32 devices in a mesh: tm: 4 (over y, x), region: 8 (over z, core).
Axes of the slice: x: 2, y: 2, z: 4, core: 2. Of those that a mesh axis runs over, the one named last changes fastest.
Arguments:
- search_one: float32 [4, 548, 8192], P('tm', None, 'region'), may hold values from -6 to 6
- search_two: float32 [4, 548, 8192], P('tm', None, 'region'), may hold values from -6 to 6
- column_gain: float32 [4, 548, 8192], P('tm', None, 'region'), may hold values from 0.5 to 1.25
- model_matrix: float32 [4, 548, 548], P('tm'), may hold values from -0.25 to 0.25
- obs_owner: int32 [4, 8192], P('tm', 'region'), may hold values from 0 to 7, as said below
- observe_matrix: float32 [4, 8, 548, 1024], P('tm', 'region'), may hold values from -0.25 to 0.25
- error_weight: float32 [4, 8, 1024], P('tm', 'region'), may hold values from 0.25 to 4
- channel_mask: int32 [4, 8, 1024], P('tm', 'region'), may hold values 0 or 1
Outputs:
- forward_state: float32 [4, 548, 8192], P('tm', None, 'region')
- gradient: float32 [4, 548, 8192], P('tm', None, 'region')
The draws below stay inside these ranges and needn't reach their ends.
Inputs may be any that keep to these rules, and one draw needn't show every extreme that they name: `obs_owner`: among the 1024 columns of one device (one subwindow, one aligned block of 1024 columns) no owner appears more than 192 times; in every subwindow one owner appears exactly 192 times in every block.
All inputs are finite; a program needn't handle non-finite values. No bound on the sum of `channel_mask` on one device may be relied on, other than what follows from the above.
Results may differ from the reference program's by a relative error of at most 0.0003.
Values sent between devices are 32-bit elements; how exact they have to be, the bound alone decides.
No kernel may reach another device: no remote copies, remote signals or barrier semaphores. Data moves between devices by JAX's collectives and lax.ppermute only.
A program may use at most 128 MiB of HBM per device.

```python
import math
import jax
import jax.numpy as jnp
from jax import lax

NV = 548
CH = 1024
COLS = 1024
COLS_TOTAL = 8192
CAP = 192
N_TM = 4
N_REGION = 8


def draw_obs_owner(key, part):
    hottest = jax.random.randint(jax.random.fold_in(key, 7), (N_TM,), 0, N_REGION)

    def one_block(index):
        owner_hot = hottest[index // N_REGION]
        block_key = jax.random.fold_in(key, index + 11)
        others = (owner_hot + 1 + jnp.arange(N_REGION - 1, dtype=jnp.int32)) % N_REGION
        pool = jnp.repeat(others, CAP)
        picked = pool[jax.random.permutation(jax.random.fold_in(block_key, 1), pool.shape[0])[:COLS - CAP]]
        whole = jnp.concatenate([jnp.full((CAP,), owner_hot, jnp.int32), picked.astype(jnp.int32)])
        return whole[jax.random.permutation(jax.random.fold_in(block_key, 2), COLS)]
    blocks = jax.vmap(one_block)(jnp.arange(N_TM * N_REGION, dtype=jnp.int32))
    return blocks.reshape(N_TM, N_REGION * COLS).astype(jnp.int32)


def touch_ends(drawn, rng, low, high):
    place = [jax.random.randint(jax.random.fold_in(rng, axis), (), 0, length) for axis, length in enumerate(drawn.shape)]
    widest = drawn.shape.index(max(drawn.shape))
    neighbour = place[:widest] + [(place[widest] + 1) % drawn.shape[widest]] + place[widest + 1:]
    return drawn.at[tuple(place)].set(low).at[tuple(neighbour)].set(high)


def block_scale(stream_key, dims, split, least, largest):
    loudness = 1.0
    for axis_at, blocks in split:
        heights = jax.random.uniform(jax.random.fold_in(jax.random.fold_in(stream_key, 6), axis_at), (blocks,), jnp.float32, least / len(split), largest / len(split))
        loudness = loudness * jnp.repeat(jnp.exp(heights), dims[axis_at] // blocks).reshape((-1,) + (1,) * (len(dims) - 1 - axis_at))
    return loudness


def centred(own_key, extent, deviation, limit, shards=(), kind=jnp.bfloat16):
    array = jax.random.normal(own_key, extent, jnp.float32) * deviation
    if len(shards) > 0:
        array = block_scale(own_key, extent, shards, -0.22, 0.18) * array
    return jnp.clip(array, min=-limit, max=limit).astype(kind)


def setup_inputs(seed: int = 0) -> dict:
    streams_of = jax.random.split(jax.random.key(seed), 9)
    search_one = centred(streams_of[0], (N_TM, NV, COLS_TOTAL), 1.0, 6.0, ((0, 4), (2, 8)), jnp.float32)
    search_two = centred(streams_of[1], (N_TM, NV, COLS_TOTAL), 1.0, 6.0, ((0, 4), (2, 8)), jnp.float32)
    column_gain = jnp.clip(jnp.exp(math.log(1.25) - 0.916290732 * jax.random.uniform(streams_of[2], (N_TM, NV, COLS_TOTAL), jnp.float32) ** block_scale(streams_of[2], (N_TM, NV, COLS_TOTAL), ((0, 4), (2, 8)), -0.2, 0.2)), 0.5, 1.25)
    model_matrix = centred(streams_of[3], (N_TM, NV, NV), NV ** -0.5, 0.25, ((0, 4),), jnp.float32)
    obs_owner = draw_obs_owner(jax.random.fold_in(streams_of[8], 71), 0)
    observe_matrix = centred(streams_of[5], (N_TM, N_REGION, NV, CH), NV ** -0.5, 0.25, ((0, 4), (1, 8)), jnp.float32)
    error_weight = jnp.clip(jnp.exp(math.log(4.0) - 2.7725887 * jax.random.uniform(streams_of[6], (N_TM, N_REGION, CH), jnp.float32) ** block_scale(streams_of[6], (N_TM, N_REGION, CH), ((0, 4), (1, 8)), -0.2, 0.2)), 0.25, 4.0)
    channel_mask = touch_ends((jax.random.randint(streams_of[7], (N_TM, N_REGION, CH), 0, 4) < 3).astype(jnp.int32), jax.random.fold_in(streams_of[7], 1), 0, 1)
    return dict(search_one=search_one, search_two=search_two, column_gain=column_gain, model_matrix=model_matrix, obs_owner=obs_owner, observe_matrix=observe_matrix, error_weight=error_weight, channel_mask=channel_mask)


def high_dot(left, right):
    return jnp.dot(left, right, precision=lax.Precision.HIGHEST, preferred_element_type=jnp.float32)


def high_tdot(left, right):
    return lax.dot_general(left, right, (((0,), (0,)), ((), ())), precision=lax.Precision.HIGHEST, preferred_element_type=jnp.float32)


def observe(state, owners, matrices, weights):
    most = N_REGION * CAP
    order = jnp.argsort(owners, stable=True).astype(jnp.int32)
    counts = jnp.sum((owners[None, :] == jnp.arange(N_REGION, dtype=jnp.int32)[:, None]).astype(jnp.int32), axis=1).astype(jnp.int32)
    starts = (jnp.cumsum(counts) - counts).astype(jnp.int32)
    padded = jnp.concatenate([order, jnp.zeros((most,), jnp.int32)])

    def one_owner(accum, inputs):
        matrix, weight, start, count = inputs
        index = lax.dynamic_slice(padded, (start,), (most,)).astype(jnp.int32)
        valid = jnp.arange(most, dtype=jnp.int32) < count
        columns = jnp.take(state, index, axis=1)
        seen = high_tdot(matrix, columns) * weight[:, None]
        back = high_dot(matrix, seen)
        back = jnp.where(valid[None, :], back, jnp.zeros_like(back))
        return accum.at[:, index].add(back), None

    result, _ = lax.scan(one_owner, jnp.zeros_like(state), (matrices, weights, starts, counts))
    return result


def reference(search_one, search_two, column_gain, model_matrix, obs_owner, observe_matrix, error_weight, channel_mask):
    forward = [search_one[0]]
    for step in range(1, N_TM):
        forward.append(search_one[step] + column_gain[step] * high_dot(model_matrix[step], forward[-1]))
    swept = [search_two[N_TM - 1]]
    for step in range(N_TM - 2, -1, -1):
        swept.insert(0, search_two[step] + high_tdot(model_matrix[step + 1], column_gain[step + 1] * swept[0]))
    weights = error_weight * channel_mask.astype(error_weight.dtype)
    gradient = []
    for step in range(N_TM):
        observed = observe(forward[step], obs_owner[step], observe_matrix[step], weights[step])
        gradient.append(swept[step] + observed)
    return jnp.stack(forward), jnp.stack(gradient)
```

```python
import functools

import jax
import jax.numpy as jnp
from jax import lax
from jax.experimental import pallas as pl
from jax.experimental.pallas import tpu as pltpu
from jax.sharding import PartitionSpec as P

LANES = 128
F32 = jnp.float32
BF16 = jnp.bfloat16
WHOLE = pl.BlockSpec(memory_space=pltpu.VMEM)
HBM = pl.BlockSpec(memory_space=pl.ANY)
SMEM = pl.BlockSpec(memory_space=pltpu.SMEM)
PARAMS = pltpu.CompilerParams(vmem_limit_bytes=56 * 1024 * 1024)


def up(size, to):
    return -(-size // to) * to


def split(x):
    high = x.astype(BF16)
    return high, (x - high.astype(F32)).astype(BF16)


def dot(left, right):
    return jnp.dot(left, right, preferred_element_type=F32)


def stack_left(ref, matrix):
    rows, size = matrix.shape
    part = up(size, 16)
    high, low = split(matrix)
    ref[...] = jnp.zeros(ref.shape, BF16)
    ref[:, 0:size] = high
    ref[:, part : part + size] = high
    ref[:, 2 * part : 2 * part + size] = low


def stack_right(ref, x):
    size = x.shape[0]
    part = up(size, 16)
    high, low = split(x)
    if part > size:
        pad = jnp.zeros((part - size, x.shape[1]), BF16)
        high = jnp.concatenate([high, pad], axis=0)
        low = jnp.concatenate([low, pad], axis=0)
    ref[0:part, :] = high
    ref[part : 2 * part, :] = low
    ref[2 * part : 3 * part, :] = high


def packing(size):
    half = size // (2 * LANES) * LANES
    rest = size - 2 * half
    across = 2 * half // LANES
    groups = up(rest, 8) // 8
    strip = half
    corner = strip + up(rest, 8)
    diagonal = corner + 8 * up(groups, across) // across
    return half, rest, across, groups, strip, corner, diagonal, diagonal + 8


def operator_kernel(h_ref, w_ref, m_ref, out_ref, left, right, full):
    size, channels = h_ref.shape
    half, rest, across, groups, strip, corner, diagonal, _ = packing(size)
    h = h_ref[...]
    weighted = h * (w_ref[...] * m_ref[...].astype(F32))
    high, low = split(weighted)
    left[:, 0:channels] = high
    left[:, channels : 2 * channels] = high
    left[:, 2 * channels : 3 * channels] = low
    high, low = split(h)
    right[:, 0:channels] = high
    right[:, channels : 2 * channels] = low
    right[:, 2 * channels : 3 * channels] = high
    full[...] = lax.dot_general(
        left[...], right[...], (((1,), (1,)), ((), ())), preferred_element_type=F32
    )
    first = full[0:half, 0:half]
    second = full[half : 2 * half, half : 2 * half]
    row = lax.broadcasted_iota(jnp.int32, (half, half), 0)
    col = lax.broadcasted_iota(jnp.int32, (half, half), 1)
    out_ref[...] = jnp.zeros(out_ref.shape, F32)
    out_ref[0:half, 0:half] = jnp.where(row <= col, first, second)
    out_ref[0:half, half : 2 * half] = full[0:half, half : 2 * half]
    out_ref[strip : strip + rest, :] = full[2 * half : size, 0 : 2 * half]
    for group in range(groups):
        at, lane = corner + 8 * (group // across), LANES * (group % across)
        take = min(8, rest - 8 * group)
        out_ref[at : at + take, lane : lane + rest] = full[
            2 * half + 8 * group : 2 * half + 8 * group + take, 2 * half : size
        ]
    out_ref[diagonal : diagonal + 1, 0:half] = jnp.sum(
        jnp.where(row == col, second, 0.0), axis=0, keepdims=True
    )


def unpack_kernel(size, packed_ref, out_ref, full):
    half, rest, across, groups, strip, corner, diagonal, _ = packing(size)
    row = lax.broadcasted_iota(jnp.int32, (half, half), 0)
    col = lax.broadcasted_iota(jnp.int32, (half, half), 1)
    both = packed_ref[0, 0:half, 0:half]
    turned = both.T
    full[0:half, 0:half] = jnp.where(row <= col, both, turned)
    ends = jnp.broadcast_to(packed_ref[0, diagonal : diagonal + 1, 0:half], (half, half))
    full[half : 2 * half, half : 2 * half] = jnp.where(
        row > col, both, jnp.where(row == col, ends, turned)
    )
    side = packed_ref[0, 0:half, half : 2 * half]
    full[0:half, half : 2 * half] = side
    full[half : 2 * half, 0:half] = side.T
    stripe = packed_ref[0, strip : strip + rest, :]
    full[2 * half : size, 0 : 2 * half] = stripe
    tall = jnp.concatenate([stripe, jnp.zeros((LANES - rest, 2 * half), F32)], axis=0).T
    full[0 : 2 * half, 2 * half : size] = tall[:, 0:rest]
    for group in range(groups):
        at, lane = corner + 8 * (group // across), LANES * (group % across)
        take = min(8, rest - 8 * group)
        full[2 * half + 8 * group : 2 * half + 8 * group + take, 2 * half : size] = packed_ref[
            0, at : at + take, lane : lane + rest
        ]
    stack_left(out_ref.at[0], full[...])


def first_kernel(pieces, here_ref, s1_ref, s2_ref, gain_ref, m_ref, *rest):
    outs, (ahead_ref, back_ref), right = rest[:pieces], rest[pieces : pieces + 2], rest[-1]
    m = m_ref[...]
    stack_left(ahead_ref, m)
    stack_left(back_ref, m.T)
    last = here_ref[0] == here_ref[1] - 1
    width = outs[0].shape[1]

    @pl.when(last)
    def _():
        for i, out in enumerate(outs):
            at = slice(i * width, (i + 1) * width)
            stack_right(right, gain_ref[:, at] * s2_ref[:, at])
            out[...] = dot(back_ref[...], right[...])

    @pl.when(jnp.logical_not(last))
    def _():
        for i, out in enumerate(outs):
            out[...] = s1_ref[:, i * width : (i + 1) * width]


def hop_kernel(stage, here_ref, in_ref, s1_ref, s2_ref, gain_ref, ahead_ref, back_ref, pay_ref, keep_ref, right):
    here = here_ref[0]

    @pl.when(here == stage)
    def _():
        stack_right(right, in_ref[...])
        pay_ref[...] = s1_ref[...] + gain_ref[...] * dot(ahead_ref[...], right[...])

    @pl.when(here == here_ref[1] - 1 - stage)
    def _():
        swept = s2_ref[...] + in_ref[...]
        keep_ref[...] = swept
        stack_right(right, gain_ref[...] * swept)
        pay_ref[...] = dot(back_ref[...], right[...])


def last_kernel(span, pieces, stages, chunk, aliased, *refs):
    here_ref, owner_ref, s1_ref, s2_ref, gain_ref, ahead_ref, g_ref = refs[:7]
    count = len(pieces)
    at = 7
    inbox = refs[at : at + count]
    at += count
    kept = []
    for _ in range(stages):
        kept.append((refs[at : at + count], refs[at + count : at + 2 * count]))
        at += 2 * count
    at += 2 if aliased else 0
    f_out, g_out = refs[at : at + 2]
    state, swept, gain, came, total, right, sems = refs[at + 2 :]
    owner = pl.program_id(0)
    here, depth = here_ref[0], here_ref[1]
    start, width = span
    piece = width // count
    edge = (here == 0) | (here == depth - 1)

    def load(copies):
        for copy in copies:
            copy.start()
        for copy in copies:
            copy.wait()

    def move(src, dst, sem):
        return pltpu.make_async_copy(src, dst, sems.at[sem])

    def parts(source, target, first):
        return [
            move(source[i], target.at[:, pl.ds(i * piece, piece)], first + i) for i in range(count)
        ]

    @pl.when(owner == 0)
    def _():
        @pl.when(edge)
        def _():
            columns = pl.ds(start, width)
            load(
                [
                    move(s1_ref.at[:, columns], state, 0),
                    move(s2_ref.at[:, columns], swept, 1),
                    move(gain_ref.at[:, columns], gain, 2),
                ]
                + parts(inbox, came, 3)
            )

        for stage in range(1, stages + 1):
            @pl.when(here == stage)
            def _():
                load(parts(kept[stage - 1][0], state, 0))

            @pl.when(here == depth - 1 - stage)
            def _():
                load(parts(kept[stage - 1][1], swept, 0))

        @pl.when(here == 0)
        def _():
            swept[...] += came[...]

        for part in range(0, width, chunk):
            columns = slice(part, part + chunk)

            @pl.when(here == depth - 1)
            def _():
                stack_right(right.at[part // chunk], came[:, columns])
                state[:, columns] += gain[:, columns] * dot(ahead_ref[...], right[part // chunk])

            stack_right(right.at[part // chunk], state[:, columns])
        total[...] = jnp.zeros(total.shape, F32)
        move(state, f_out.at[:, pl.ds(start, width)], 0).start()

    for part in range(0, width, chunk):
        columns = slice(part, part + chunk)
        seen = dot(g_ref[0], right[part // chunk])
        mine = owner_ref[:, columns] == owner
        total[:, columns] = jnp.where(mine, seen, total[:, columns])

    @pl.when(owner == pl.num_programs(0) - 1)
    def _():
        total[...] += swept[...]
        move(state, f_out.at[:, pl.ds(start, width)], 0).wait()
        load([move(total, g_out.at[:, pl.ds(start, width)], 1)])


def body(search_one, search_two, column_gain, model_matrix, obs_owner, observe_matrix, error_weight, channel_mask):
    depth = lax.axis_size("tm")
    regions = lax.axis_size("region")
    s1, s2, gain, matrix = search_one[0], search_two[0], column_gain[0], model_matrix[0]
    size, columns = s1.shape
    channels = observe_matrix.shape[3]
    here = jnp.stack([lax.axis_index("tm"), jnp.int32(depth)]).astype(jnp.int32)
    width = LANES
    pieces = columns // width
    stages = depth - 2
    stacked = 3 * up(size, 16)
    top = depth - 1

    def sent(x, *hops):
        return lax.ppermute(x, "tm", list(hops))

    first = pl.pallas_call(
        functools.partial(first_kernel, pieces),
        out_shape=[jax.ShapeDtypeStruct((size, width), F32)] * pieces
        + [jax.ShapeDtypeStruct((size, stacked), BF16)] * 2,
        in_specs=[SMEM] + [WHOLE] * 4,
        out_specs=[WHOLE] * (pieces + 2),
        scratch_shapes=[pltpu.VMEM((stacked, width), BF16)],
        compiler_params=PARAMS,
        name="first",
    )(here, s1, s2, gain, matrix)
    pay, ahead, back = list(first[:pieces]), first[pieces], first[pieces + 1]

    rows = packing(size)[-1]
    half = packing(size)[0]
    packed = pl.pallas_call(
        operator_kernel,
        out_shape=jax.ShapeDtypeStruct((rows, 2 * half), F32),
        in_specs=[WHOLE] * 3,
        out_specs=WHOLE,
        scratch_shapes=[pltpu.VMEM((size, 3 * channels), BF16)] * 2 + [pltpu.VMEM((size, size), F32)],
        compiler_params=PARAMS,
        name="operator",
    )(observe_matrix[0, 0], error_weight[0], channel_mask[0])
    gathered = lax.all_gather(packed, "region")
    operators = pl.pallas_call(
        functools.partial(unpack_kernel, size),
        grid=(regions,),
        out_shape=jax.ShapeDtypeStruct((regions, size, stacked), BF16),
        in_specs=[pl.BlockSpec((1, rows, 2 * half), lambda o: (o, 0, 0))],
        out_specs=pl.BlockSpec((1, size, stacked), lambda o: (o, 0, 0)),
        scratch_shapes=[pltpu.VMEM((size, size), F32)],
        compiler_params=PARAMS,
        name="unpack",
    )(gathered)

    def hop(stage, i, came):
        block = pl.BlockSpec((size, width), lambda _: (0, i))
        whole = pl.BlockSpec((size, width), lambda _: (0, 0))
        matrices = pl.BlockSpec((size, stacked), lambda _: (0, 0))
        return pl.pallas_call(
            functools.partial(hop_kernel, stage),
            grid=(1,),
            out_shape=[jax.ShapeDtypeStruct((size, width), F32)] * 2,
            in_specs=[SMEM, whole, block, block, block, matrices, matrices],
            out_specs=[whole] * 2,
            scratch_shapes=[pltpu.VMEM((stacked, width), BF16)],
            compiler_params=PARAMS,
            cost_estimate=pl.CostEstimate(flops=2 * size * stacked * width, bytes_accessed=6 * size * width * 4, transcendentals=0),
            name="hop",
        )(here, came, s1, s2, gain, ahead, back)

    detour = set(range(pieces // 2, pieces))
    kept = [[], []]
    inbox = [[None] * pieces for _ in range(depth)]
    store = [[None] * pieces for _ in range(depth)]
    for i in range(pieces):
        out = pay[i]
        for stage in range(1, depth):
            low, high = stage - 1, depth - stage
            if 0 < low < top - 1 and i in detour:
                out = sent(out, (low, low + 2), (high, high - 2))
                came = sent(out, (low + 2, low + 1), (high - 2, high - 1))
            else:
                came = sent(out, (low, low + 1), (high, high - 1))
            inbox[stage][i] = came
            if stage < top:
                out, keep = hop(stage, i, came)
                store[stage][i] = (out, keep)

    owners = obs_owner
    chunk = 2 * width
    done = None
    for begin, end in ((0, pieces - 2), (pieces - 2, pieces)):
        span = (begin * width, (end - begin) * width)
        count = end - begin
        chosen = list(range(begin, end))
        operands = [here, owners[:, span[0] : span[0] + span[1]], s1, s2, gain, ahead, operators]
        specs = [SMEM, WHOLE, HBM, HBM, HBM, WHOLE, pl.BlockSpec((1, size, stacked), lambda o: (o, 0, 0))]
        operands += [inbox[top][i] for i in chosen]
        for stage in range(1, depth - 1):
            operands += [store[stage][i][0] for i in chosen]
            operands += [store[stage][i][1] for i in chosen]
        aliases = {}
        if done is not None:
            aliases = {len(operands): 0, len(operands) + 1: 1}
            operands += list(done)
        specs += [HBM] * (len(operands) - len(specs))
        done = pl.pallas_call(
            functools.partial(last_kernel, span, chosen, stages, chunk, done is not None),
            grid=(regions,),
            out_shape=[jax.ShapeDtypeStruct((size, columns), F32)] * 2,
            in_specs=specs,
            out_specs=[HBM] * 2,
            scratch_shapes=[pltpu.VMEM((size, span[1]), F32)] * 5
            + [pltpu.VMEM((span[1] // chunk, stacked, chunk), BF16), pltpu.SemaphoreType.DMA((3 + count,))],
            input_output_aliases=aliases,
            compiler_params=PARAMS,
            cost_estimate=pl.CostEstimate(flops=2 * size * stacked * span[1] * regions, bytes_accessed=regions * size * stacked * 2, transcendentals=0),
            name="last",
        )(*operands)
    return done[0][None], done[1][None]


def solution(mesh):
    return jax.shard_map(
        body,
        mesh=mesh,
        in_specs=(
            P("tm", None, "region"),
            P("tm", None, "region"),
            P("tm", None, "region"),
            P("tm", None, None),
            P("tm", "region"),
            P("tm", "region", None, None),
            P("tm", "region", None),
            P("tm", "region", None),
        ),
        out_specs=(P("tm", None, "region"), P("tm", None, "region")),
        check_vma=False,
    )
```

```python
import functools

import jax
import jax.numpy as jnp
from jax import lax
from jax.experimental import pallas as pl
from jax.experimental.pallas import tpu as pltpu
from jax.sharding import PartitionSpec as P

LANES = 128
F32 = jnp.float32
BF16 = jnp.bfloat16
WHOLE = pl.BlockSpec(memory_space=pltpu.VMEM)
ANY = pl.BlockSpec(memory_space=pl.ANY)
HBM = pl.BlockSpec(memory_space=pltpu.HBM)


def pinned(x):
    return pltpu.with_memory_space_constraint(x, pltpu.HBM)


def params(mebibytes):
    return pltpu.CompilerParams(vmem_limit_bytes=mebibytes * 1024 * 1024)


def cost(flops, touched):
    return pl.CostEstimate(flops=int(flops), bytes_accessed=int(touched), transcendentals=0)


def up(size, to):
    return -(-size // to) * to


def split(x):
    high = x.astype(BF16)
    return high, (x - high.astype(F32)).astype(BF16)


def dot(left, right):
    return jnp.dot(left, right, preferred_element_type=F32)


def stack_left(ref, matrix):
    rows, size = matrix.shape
    part = up(size, 16)
    high, low = split(matrix)
    ref[...] = jnp.zeros(ref.shape, BF16)
    ref[:, 0:size] = high
    ref[:, part : part + size] = high
    ref[:, 2 * part : 2 * part + size] = low


def padded(x):
    size = x.shape[0]
    part = up(size, 16)
    if part == size:
        return x
    return jnp.concatenate([x, jnp.zeros((part - size, x.shape[1]), x.dtype)], axis=0)


def stack_right(ref, x):
    part = up(x.shape[0], 16)
    high, low = split(x)
    high = padded(high)
    ref[0:part, :] = high
    ref[part : 2 * part, :] = padded(low)
    ref[2 * part : 3 * part, :] = high


def columns_of(source, width, piece):
    return source.at[:, 0, piece * width : (piece + 1) * width]


def load(copies):
    for copy in copies:
        copy.start()
    for copy in copies:
        copy.wait()


def packing(size):
    half = size // (2 * LANES) * LANES
    rest = size - 2 * half
    across = 2 * half // LANES
    groups = up(rest, 8) // 8
    strip = half
    corner = strip + up(rest, 8)
    diagonal = corner + 8 * up(groups, across) // across
    return half, rest, across, groups, strip, corner, diagonal, diagonal + 8


def operator_kernel(after, h_hbm, w_hbm, m_hbm, out_ref, h_ref, w_ref, m_ref, left, right, full, sems):
    size, channels = h_ref.shape
    half, rest, across, groups, strip, corner, diagonal, _ = packing(size)
    load(
        [
            pltpu.make_async_copy(h_hbm.at[:, 0, :], h_ref, sems.at[0]),
            pltpu.make_async_copy(w_hbm, w_ref, sems.at[1]),
            pltpu.make_async_copy(m_hbm, m_ref, sems.at[2]),
        ]
    )
    h = h_ref[...]
    high, low = split(h * (w_ref[...] * m_ref[...].astype(F32)))
    left[:, 0:channels] = high
    left[:, channels : 2 * channels] = high
    left[:, 2 * channels : 3 * channels] = low
    high, low = split(h)
    right[:, 0:channels] = high
    right[:, channels : 2 * channels] = low
    right[:, 2 * channels : 3 * channels] = high
    full[...] = lax.dot_general(
        left[...], right[...], (((1,), (1,)), ((), ())), preferred_element_type=F32
    )
    first = full[0:half, 0:half]
    second = full[half : 2 * half, half : 2 * half]
    row = lax.broadcasted_iota(jnp.int32, (half, half), 0)
    col = lax.broadcasted_iota(jnp.int32, (half, half), 1)
    out_ref[strip:, :] = jnp.zeros((out_ref.shape[0] - strip, out_ref.shape[1]), F32)
    out_ref[0:half, 0:half] = jnp.where(row <= col, first, second)
    out_ref[0:half, half : 2 * half] = full[0:half, half : 2 * half]
    out_ref[strip : strip + rest, :] = full[2 * half : size, 0 : 2 * half]
    for group in range(groups):
        at, lane = corner + 8 * (group // across), LANES * (group % across)
        take = min(8, rest - 8 * group)
        out_ref[at : at + take, lane : lane + rest] = full[
            2 * half + 8 * group : 2 * half + 8 * group + take, 2 * half : size
        ]
    out_ref[diagonal : diagonal + 1, 0:half] = jnp.sum(
        jnp.where(row == col, second, 0.0), axis=0, keepdims=True
    )


def unpack_kernel(size, after, packed_hbm, out_ref, full, slots, sems):
    half, rest, across, groups, strip, corner, diagonal, _ = packing(size)
    owner = pl.program_id(0)
    if full.shape[1] > size:
        full[:, size:] = jnp.zeros((size, full.shape[1] - size), F32)

    def fetch(which):
        slot = lax.rem(which, 2)
        return pltpu.make_async_copy(packed_hbm.at[which], slots.at[slot], sems.at[slot])

    @pl.when(owner == 0)
    def _():
        fetch(owner).start()

    @pl.when(owner + 1 < pl.num_programs(0))
    def _():
        fetch(owner + 1).start()

    fetch(owner).wait()
    packed_ref = slots.at[lax.rem(owner, 2)]
    row = lax.broadcasted_iota(jnp.int32, (half, half), 0)
    col = lax.broadcasted_iota(jnp.int32, (half, half), 1)
    both = packed_ref[0:half, 0:half]
    turned = both.T
    full[0:half, 0:half] = jnp.where(row <= col, both, turned)
    ends = jnp.broadcast_to(packed_ref[diagonal : diagonal + 1, 0:half], (half, half))
    full[half : 2 * half, half : 2 * half] = jnp.where(
        row > col, both, jnp.where(row == col, ends, turned)
    )
    side = packed_ref[0:half, half : 2 * half]
    full[0:half, half : 2 * half] = side
    full[half : 2 * half, 0:half] = side.T
    stripe = packed_ref[strip : strip + rest, :]
    full[2 * half : size, 0 : 2 * half] = stripe
    tall = jnp.concatenate([stripe, jnp.zeros((LANES - rest, 2 * half), F32)], axis=0).T
    full[0 : 2 * half, 2 * half : size] = tall[:, 0:rest]
    for group in range(groups):
        at, lane = corner + 8 * (group // across), LANES * (group % across)
        take = min(8, rest - 8 * group)
        full[2 * half + 8 * group : 2 * half + 8 * group + take, 2 * half : size] = packed_ref[
            at : at + take, lane : lane + rest
        ]
    part = full.shape[1]
    high, low = split(full[...])
    out_ref[0, :, 0:part] = high
    out_ref[0, :, part : 2 * part] = high
    out_ref[0, :, 2 * part : 3 * part] = low


def first_kernel(begin, count, depth, after, s1_hbm, s2_hbm, gain_hbm, m_hbm, *rest):
    early = begin == 0
    pay = rest[1 - early : 1 - early + count]
    matrix_ref, m_ref, s2, gain, right, sems = rest[1 - early + count :]
    here = lax.axis_index("tm")
    width = pay[0].shape[1]
    back = matrix_ref if early else rest[0]

    def fetch(source, targets, which):
        return [
            pltpu.make_async_copy(
                columns_of(source, width, begin + i), targets[i], sems.at[which * count + i]
            )
            for i in range(count)
        ]

    @pl.when(here == 0)
    def _():
        load(fetch(s1_hbm, pay, 0))

    @pl.when(here > 0)
    def _():
        matrix = pltpu.make_async_copy(m_hbm.at[:, 0, :], m_ref, sems.at[2 * count])
        matrix.start()

        @pl.when(here == depth - 1)
        def _():
            copies = fetch(s2_hbm, [s2.at[i] for i in range(count)], 0)
            copies += fetch(gain_hbm, [gain.at[i] for i in range(count)], 1)
            for copy in copies:
                copy.start()

        matrix.wait()
        stack_left(matrix_ref, m_ref[...].T if early else m_ref[...])

        @pl.when(here == depth - 1)
        def _():
            copies = fetch(s2_hbm, [s2.at[i] for i in range(count)], 0)
            copies += fetch(gain_hbm, [gain.at[i] for i in range(count)], 1)
            for copy in copies:
                copy.wait()
            for i in range(count):
                stack_right(right, gain[i] * s2[i])
                pay[i][...] = dot(back[...], right[...])


def hop_kernel(stage, depth, piece, after, s1_hbm, s2_hbm, gain_hbm, in_ref, ahead_ref, back_ref, *rest):
    edge, (pay_ref, keep_hbm, source, gain, kept, right, sems) = rest[:-7], rest[-7:]
    here = lax.axis_index("tm")
    width = pay_ref.shape[1]

    def fetch(hbm, target, which):
        copy = pltpu.make_async_copy(columns_of(hbm, width, piece), target, sems.at[which])
        copy.start()
        return copy

    if edge:
        @pl.when((here == 0) | (here == depth - 1))
        def _():
            pay_ref[...] = edge[0][...]

    @pl.when(here == stage)
    def _():
        copies = fetch(s1_hbm, source, 0), fetch(gain_hbm, gain, 1)
        stack_right(right, in_ref[...])
        moved = dot(ahead_ref[...], right[...])
        for copy in copies:
            copy.wait()
        state = source[...] + gain[...] * moved
        pay_ref[...] = state
        kept[...] = state
        load([pltpu.make_async_copy(kept, keep_hbm, sems.at[2])])

    @pl.when(here == depth - 1 - stage)
    def _():
        copies = fetch(s2_hbm, source, 0), fetch(gain_hbm, gain, 1)
        for copy in copies:
            copy.wait()
        swept = source[...] + in_ref[...]
        kept[...] = swept
        out = pltpu.make_async_copy(kept, keep_hbm, sems.at[2])
        out.start()
        stack_right(right, gain[...] * swept)
        pay_ref[...] = dot(back_ref[...], right[...])
        out.wait()


def last_kernel(piece, depth, regions, aliased, after, owner_ref, ahead_hbm, g_ref, s1_hbm, s2_hbm, gain_hbm, inbox, *refs):
    kept, refs = refs[: depth - 2], refs[depth - 2 + 2 * aliased :]
    f_out, g_out, token, state, swept, gain, came, total, ahead, small, right, slots, sems = refs
    token[...] = jnp.zeros(token.shape, F32)
    here = lax.axis_index("tm")
    size, width = total.shape
    part = right.shape[0] // 3
    resident = slots.shape[0] == 1

    def copy(source, target, which):
        return pltpu.make_async_copy(source, target, sems.at[which])

    def window(source):
        return columns_of(source, width, piece)

    def fetch(which):
        slot = lax.rem(which, 2)
        return copy(g_ref.at[which], slots.at[slot], 5 + slot)

    if not resident:
        fetch(0).start()

    @pl.when(here == 0)
    def _():
        load([copy(window(s1_hbm), state, 0), copy(window(s2_hbm), swept, 1), copy(inbox, came, 2)])
        swept[...] += came[...]

    for stage in range(1, depth - 1):
        @pl.when(here == stage)
        def _():
            load([copy(kept[stage - 1], state, 0), copy(kept[depth - 2 - stage], swept, 1)])

    @pl.when(here == depth - 1)
    def _():
        load(
            [
                copy(window(s1_hbm), state, 0),
                copy(window(s2_hbm), swept, 1),
                copy(inbox, came, 2),
                copy(window(gain_hbm), gain, 3),
                copy(ahead_hbm, ahead, 4),
            ]
        )
        stack_right(small, came[...])
        state[...] += gain[...] * dot(ahead[...], small[...])

    kept_state = copy(state, window(f_out), 0)
    kept_state.start()
    high, low = split(state[...])
    short = up(size, 16)
    for at, term in ((0, high), (part, low), (2 * part, high)):
        right[at : at + short, :] = padded(term)
        if part > short:
            right[at + short : at + part, :] = jnp.zeros((part - short, width), BF16)
    total[...] = swept[...]
    owners = owner_ref[:, piece * width : (piece + 1) * width]

    def one_owner(owner, carry):
        if resident:
            g = g_ref.at[owner]
        else:
            @pl.when(owner + 1 < regions)
            def _():
                fetch(owner + 1).start()

            fetch(owner).wait()
            g = slots.at[lax.rem(owner, 2)]
        seen = dot(g[...], right[...])
        total[...] += jnp.where(owners == owner, seen, 0.0)
        return carry

    lax.fori_loop(0, regions, one_owner, 0)
    kept_state.wait()
    load([copy(total, window(g_out), 1)])


def body(search_one, search_two, column_gain, model_matrix, obs_owner, observe_matrix, error_weight, channel_mask):
    depth = lax.axis_size("tm")
    regions = lax.axis_size("region")
    size, columns = search_one.shape[1:]
    channels = observe_matrix.shape[3]
    s1, s2, gain = (pinned(x.reshape(size, 1, columns)) for x in (search_one, search_two, column_gain))
    matrix = pinned(model_matrix.reshape(size, 1, size))
    observe = pinned(observe_matrix.reshape(size, 1, channels))
    width = 2 * LANES
    pieces = columns // width
    part, wide = up(size, 16), up(size, LANES)
    top = depth - 1
    held = pltpu.VMEM((size, width), F32)
    ones = size * width

    def sent(x, *hops):
        return lax.ppermute(x, "tm", list(hops))

    def first(after, begin, end, *back):
        count = end - begin
        return pl.pallas_call(
            functools.partial(first_kernel, begin, count, depth),
            out_shape=[held] * count + [pltpu.VMEM((size, 3 * part), BF16)],
            in_specs=[ANY] + [HBM] * 4 + [WHOLE] * len(back),
            out_specs=[WHOLE] * (count + 1),
            scratch_shapes=[
                pltpu.VMEM((size, size), F32),
                pltpu.VMEM((count, size, width), F32),
                pltpu.VMEM((count, size, width), F32),
                pltpu.VMEM((3 * part, width), BF16),
                pltpu.SemaphoreType.DMA((2 * count + 1,)),
            ],
            compiler_params=params(24),
            cost_estimate=cost(6 * size * count * ones, 24 * count * ones),
            name="first",
        )(after, s1, s2, gain, matrix, *back)

    half, rows = packing(size)[0], packing(size)[-1]
    *pay, back = first(s1, 0, 1)
    packed = pl.pallas_call(
        operator_kernel,
        out_shape=pltpu.HBM((rows, 2 * half), F32),
        in_specs=[ANY] + [HBM] * 3,
        out_specs=WHOLE,
        scratch_shapes=[
            pltpu.VMEM((size, channels), F32),
            pltpu.VMEM((1, channels), F32),
            pltpu.VMEM((1, channels), jnp.int32),
            pltpu.VMEM((size, 3 * channels), BF16),
            pltpu.VMEM((size, 3 * channels), BF16),
            pltpu.VMEM((size, size), F32),
            pltpu.SemaphoreType.DMA((3,)),
        ],
        compiler_params=params(24),
        cost_estimate=cost(6 * size * size * channels, 8 * size * channels),
        name="operator",
    )(back, observe, pinned(error_weight[0]), pinned(channel_mask[0]))
    gathered = lax.all_gather(packed, "region")
    *others, ahead = first(pinned(packed), 1, pieces, back)
    pay += others

    def unpack(after):
        return pl.pallas_call(
            functools.partial(unpack_kernel, size),
            grid=(regions,),
            out_shape=jax.ShapeDtypeStruct((regions, size, 3 * wide), BF16),
            in_specs=[ANY, HBM],
            out_specs=pl.BlockSpec((1, size, 3 * wide), lambda o: (o, 0, 0)),
            scratch_shapes=[
                pltpu.VMEM((size, wide), F32),
                pltpu.VMEM((2, rows, 2 * half), F32),
                pltpu.SemaphoreType.DMA((2,)),
            ],
            compiler_params=params(16),
            cost_estimate=cost(0, regions * size * size * 8),
            name="unpack",
        )(after, pinned(gathered))

    def hop(after, stage, i, came, *edge):
        return pl.pallas_call(
            functools.partial(hop_kernel, stage, depth, i),
            out_shape=[held, pltpu.HBM((size, width), F32)],
            in_specs=[ANY] + [HBM] * 3 + [WHOLE] * (3 + len(edge)),
            out_specs=[WHOLE, HBM],
            scratch_shapes=[pltpu.VMEM((size, width), F32)] * 3
            + [pltpu.VMEM((3 * part, width), BF16), pltpu.SemaphoreType.DMA((3,))],
            compiler_params=params(12),
            cost_estimate=cost(180 * size * ones, 24 * ones),
            name="hop",
        )(after, s1, s2, gain, came, ahead, back, *edge)

    resident = regions * size * 6 * wide <= 20 * 1024 * 1024

    def last(after, i, done):
        operands = [after, obs_owner, ahead, operators, s1, s2, gain, inbox[top, i]]
        specs = [ANY, WHOLE, ANY, WHOLE if resident else ANY, HBM, HBM, HBM, ANY]
        operands += [store[stage, i] for stage in range(1, top)]
        aliases = {}
        if done is not None:
            aliases = {len(operands): 0, len(operands) + 1: 1}
            operands += list(done)
        specs += [HBM] * (len(operands) - len(specs))
        slots = (1, 16, LANES) if resident else (2, size, 3 * wide)
        return pl.pallas_call(
            functools.partial(last_kernel, i, depth, regions, done is not None),
            out_shape=[pltpu.HBM((size, 1, columns), F32)] * 2 + [jax.ShapeDtypeStruct((8, LANES), F32)],
            in_specs=specs,
            out_specs=[HBM] * 2 + [WHOLE],
            scratch_shapes=[pltpu.VMEM((size, width), F32)] * 5
            + [
                pltpu.VMEM((size, 3 * part), BF16),
                pltpu.VMEM((3 * part, width), BF16),
                pltpu.VMEM((3 * wide, width), BF16),
                pltpu.VMEM(slots, BF16),
                pltpu.SemaphoreType.DMA((7,)),
            ],
            input_output_aliases=aliases,
            compiler_params=params(12 if resident else 24),
            cost_estimate=cost(6 * size * ones * regions, 4 * regions * size * part),
            name="last",
        )(*operands)

    inbox, store = {}, {}
    detour = pieces // 2
    outward = [(i, 1) for i in range(pieces)] + [(i, 2) for i in range(detour, pieces)]
    alone = len(outward) - (pieces - 1)
    aside = {}

    def link(low, by=1):
        high = top - low
        return [(low, low + by), (high, high - by)]

    def send_middle(i, out):
        if i < detour:
            inbox[2, i] = sent(out, *link(1))
        else:
            aside[i] = sent(out, *link(1, 2))

    for i, _ in outward[:alone]:
        inbox[1, i] = sent(pay[i], *link(0))
    after = ahead
    operators = done = None
    order = [("q", 0), ("q", 1), ("r", 0), ("q", 2), ("r", 1), ("q", 3), ("r", 2), ("u", 0), ("t", 0), ("r", 3), ("t", 1), ("t", 2), ("t", 3)]
    for kind, i in order:
        if kind == "q":
            out, after = hop(after, 1, i, inbox[1, i])
            after = store[1, i] = pinned(after)
            send_middle(i, out)
        elif kind == "r":
            follow = outward[alone + i] if alone + i < len(outward) else None
            edge = () if follow is None else ((pay if follow[1] == 1 else aside)[follow[0]],)
            out, after = hop(after, 2, i, inbox[2, i], *edge)
            after = store[2, i] = pinned(after)
            if follow is None:
                inbox[3, i] = sent(out, *link(2))
            else:
                inbox[3, i] = inbox[follow[1], follow[0]] = sent(out, *link(0), *link(2))
        elif kind == "u":
            operators = unpack(after)
        else:
            *done, after = last(after, i, done)
    return tuple(x.reshape(1, size, columns) for x in done)


def solution(mesh):
    return jax.shard_map(
        body,
        mesh=mesh,
        in_specs=(
            P("tm", None, "region"),
            P("tm", None, "region"),
            P("tm", None, "region"),
            P("tm", None, None),
            P("tm", "region"),
            P("tm", "region", None, None),
            P("tm", "region", None),
            P("tm", "region", None),
        ),
        out_specs=(P("tm", None, "region"), P("tm", None, "region")),
        check_vma=False,
    )
```

```python
import functools

import jax
import jax.numpy as jnp
from jax import lax
from jax.experimental import pallas as pl
from jax.experimental.pallas import tpu as pltpu
from jax.sharding import PartitionSpec as P

LANES = 128
F32 = jnp.float32
BF16 = jnp.bfloat16
WHOLE = pl.BlockSpec(memory_space=pltpu.VMEM)
ANY = pl.BlockSpec(memory_space=pl.ANY)
HBM = pl.BlockSpec(memory_space=pltpu.HBM)


def far(x):
    return pltpu.with_memory_space_constraint(x, pltpu.HBM)


def near(x):
    return pltpu.with_memory_space_constraint(x, pltpu.VMEM)


def params(mebibytes):
    return pltpu.CompilerParams(vmem_limit_bytes=mebibytes * 1024 * 1024)


def cost(flops, touched):
    return pl.CostEstimate(flops=int(flops), bytes_accessed=int(touched), transcendentals=0)


def up(size, to):
    return -(-size // to) * to


def split(x):
    high = x.astype(BF16)
    return high, (x - high.astype(F32)).astype(BF16)


def dot(left, right):
    return jnp.dot(left, right, preferred_element_type=F32)


def stacking(size):
    main = size // LANES * LANES
    rest = size - main
    return main, rest, up(rest, 16)


def stacked(size):
    main, _, room = stacking(size)
    return 3 * (main + room)


def stack_left(ref, matrix):
    main, rest, room = stacking(matrix.shape[1])
    if room > rest:
        ref[:, 3 * main :] = jnp.zeros((matrix.shape[0], 3 * room), BF16)
    for k, term in enumerate(split(matrix)):
        for at in (0, 1) if k == 0 else (2,):
            ref[:, at * main : (at + 1) * main] = term[:, 0:main]
            if rest:
                start = 3 * main + at * room
                ref[:, start : start + rest] = term[:, main : main + rest]


def stack_right(ref, x):
    main, rest, room = stacking(x.shape[0])
    for k, term in enumerate(split(x)):
        end = term[main : main + rest, :]
        if room > rest:
            end = jnp.concatenate([end, jnp.zeros((room - rest, x.shape[1]), BF16)], axis=0)
        for at in (0, 2) if k == 0 else (1,):
            ref[at * main : (at + 1) * main, :] = term[0:main, :]
            if rest:
                start = 3 * main + at * room
                ref[start : start + room, :] = end


def columns_of(source, width, piece):
    return source.at[:, 0, piece * width : (piece + 1) * width]


def load(copies):
    for copy in copies:
        copy.start()
    for copy in copies:
        copy.wait()


def packing(size):
    half = size // (2 * LANES) * LANES
    rest = size - 2 * half
    cell = LANES // 2 if rest <= LANES // 2 else LANES
    across = 2 * half // cell
    strip = half
    corner = strip + up(rest + 1, 8)
    height = corner + 8 * (up(up(rest, 8) // 8, across) // across)
    cells = [
        (8 * g, min(8, rest - 8 * g), corner + 8 * (g // across), cell * (g % across))
        for g in range(up(rest, 8) // 8)
    ]
    return half, rest, cells, strip, strip + rest, height


def operator_kernel(after, h_hbm, w_hbm, m_hbm, copies_hbm, out_ref, h_ref, w_ref, m_ref, left, right, full, sems):
    size, channels = h_ref.shape
    half, rest, cells, strip, diagonal, _ = packing(size)
    load(
        [
            pltpu.make_async_copy(h_hbm.at[:, 0, :], h_ref, sems.at[0]),
            pltpu.make_async_copy(w_hbm, w_ref, sems.at[1]),
            pltpu.make_async_copy(m_hbm, m_ref, sems.at[2]),
        ]
    )
    h = h_ref[...]
    high, low = split(h * (w_ref[...] * m_ref[...].astype(F32)))
    left[:, 0:channels] = high
    left[:, channels : 2 * channels] = high
    left[:, 2 * channels : 3 * channels] = low
    high, low = split(h)
    right[:, 0:channels] = high
    right[:, channels : 2 * channels] = low
    right[:, 2 * channels : 3 * channels] = high
    full[...] = lax.dot_general(
        left[...], right[...], (((1,), (1,)), ((), ())), preferred_element_type=F32
    )
    first = full[0:half, 0:half]
    second = full[half : 2 * half, half : 2 * half]
    row = lax.broadcasted_iota(jnp.int32, (half, half), 0)
    col = lax.broadcasted_iota(jnp.int32, (half, half), 1)
    out_ref[strip:, :] = jnp.zeros((out_ref.shape[0] - strip, out_ref.shape[1]), F32)
    out_ref[0:half, 0:half] = jnp.where(row <= col, first, second)
    out_ref[0:half, half : 2 * half] = full[0:half, half : 2 * half]
    out_ref[strip : strip + rest, :] = full[2 * half : size, 0 : 2 * half]
    for row_at, take, at, lane in cells:
        out_ref[at : at + take, lane : lane + rest] = full[
            2 * half + row_at : 2 * half + row_at + take, 2 * half : size
        ]
    out_ref[diagonal : diagonal + 1, 0:half] = jnp.sum(
        jnp.where(row == col, second, 0.0), axis=0, keepdims=True
    )
    if len(copies_hbm.shape) == 2:
        load([pltpu.make_async_copy(out_ref, copies_hbm, sems.at[0])])
    else:
        load([pltpu.make_async_copy(out_ref, copies_hbm.at[k], sems.at[k]) for k in range(copies_hbm.shape[0])])


def make_unit(unit, turn):
    row = lax.broadcasted_iota(jnp.int32, unit.shape, 0)
    col = lax.broadcasted_iota(jnp.int32, unit.shape, 1)
    unit[...] = jnp.where(row == col, 1.0, 0.0).astype(BF16)
    turn[...] = jnp.zeros(turn.shape, BF16)


def unpack_kernel(other, size, after, packed_hbm, *refs):
    out_ref, slots, turn, unit, sems = [*refs[other:][:1], *refs[-4:]]
    kind = lax.rem(lax.axis_index("region") + other, 2)
    pairs = slots.shape[0]

    def fetch(k):
        return pltpu.make_async_copy(packed_hbm.at[k], slots.at[k], sems.at[k])

    for k in range(pairs):
        fetch(k).start()
    make_unit(unit, turn)
    for k in range(pairs):
        fetch(k).wait()

    def one_block(k, carry):
        unfold(size, slots.at[k], out_ref.at[2 * k + kind], turn, unit)
        return carry

    lax.fori_loop(0, pairs, one_block, 0)


def unpack_all_kernel(regions, after, packed_hbm, out_hbm, slots, turn, unit, stacks, sems):
    make_unit(unit, turn)

    def fetch(which):
        slot = lax.rem(which, 2)
        return pltpu.make_async_copy(packed_hbm.at[which], slots.at[slot], sems.at[slot])

    def one_owner(owner, carry):
        @pl.when(owner + 1 < regions)
        def _():
            fetch(owner + 1).start()

        fetch(owner).wait()
        unfold(stacks.shape[0], slots.at[lax.rem(owner, 2)], stacks, turn, unit)
        load([pltpu.make_async_copy(stacks, out_hbm.at[owner], sems.at[2])])
        return carry

    fetch(0).start()
    lax.fori_loop(0, regions, one_owner, 0)


def unfold(size, packed_ref, out_ref, turn, unit):
    half, rest, cells, strip, diagonal, _ = packing(size)
    main, over, room = stacking(size)
    gap = up(rest, 16)
    square = split(packed_ref[0:half, 0:half])
    side = split(packed_ref[0:half, half : 2 * half])
    stripe = split(packed_ref[strip : strip + rest, :])
    for k in range(2):
        turn[k * half : (k + 1) * half, :] = square[k]
        turn[(2 + k) * half : (3 + k) * half, :] = side[k]
        for j in range(2):
            at = 4 * half + (2 * k + j) * gap
            turn[at : at + rest, :] = stripe[k][:, j * half : (j + 1) * half]
    turned = lax.dot_general(
        unit[...], turn[...], (((1,), (1,)), ((), ())), preferred_element_type=F32
    )
    row = lax.broadcasted_iota(jnp.int32, (half, half), 0)
    col = lax.broadcasted_iota(jnp.int32, (half, half), 1)
    ends = split(packed_ref[diagonal : diagonal + 1, 0:half])
    if room > over:
        out_ref[:, 3 * main :] = jnp.zeros((size, 3 * room), BF16)

    def put(k, rows, columns, value):
        for at in (0, 1) if k == 0 else (2,):
            if columns < main:
                out_ref[rows : rows + value.shape[0], at * main + columns : at * main + columns + value.shape[1]] = value
            else:
                start = 3 * main + at * room
                out_ref[rows : rows + value.shape[0], start : start + value.shape[1]] = value

    for k in range(2):
        here = square[k].astype(F32)
        there = turned[:, k * half : (k + 1) * half]
        put(k, 0, 0, jnp.where(row <= col, here, there).astype(BF16))
        end = jnp.broadcast_to(ends[k].astype(F32), (half, half))
        put(k, half, half, jnp.where(row > col, here, jnp.where(row == col, end, there)).astype(BF16))
        put(k, 0, half, side[k])
        put(k, half, 0, turned[:, (2 + k) * half : (3 + k) * half].astype(BF16))
        put(k, 2 * half, 0, stripe[k])
        for j in range(2):
            at = 4 * half + (2 * k + j) * gap
            put(k, j * half, 2 * half, turned[:, at : at + rest].astype(BF16))
    for row_at, take, at, lane in cells:
        corner = split(packed_ref[at : at + take, lane : lane + rest])
        for k in range(2):
            put(k, 2 * half + row_at, 2 * half, corner[k])


def first_kernel(depth, s1_hbm, s2_hbm, gain_hbm, m_hbm, pay, back, m_ref, s2, gain, right, sems):
    here = lax.axis_index("tm")
    width = pay.shape[1]

    @pl.when(here == 0)
    def _():
        load([pltpu.make_async_copy(columns_of(s1_hbm, width, 0), pay, sems.at[0])])

    @pl.when(here == depth - 1)
    def _():
        load(
            [
                pltpu.make_async_copy(m_hbm.at[:, 0, :], m_ref, sems.at[0]),
                pltpu.make_async_copy(columns_of(s2_hbm, width, 0), s2, sems.at[1]),
                pltpu.make_async_copy(columns_of(gain_hbm, width, 0), gain, sems.at[2]),
            ]
        )
        stack_left(back, m_ref[...].T)
        stack_right(right, gain[...] * s2[...])
        pay[...] = dot(back[...], right[...])


def rest_kernel(pieces, depth, after, s1_hbm, s2_hbm, gain_hbm, m_hbm, ahead, back, *rest):
    cut, pay = rest[: 3 * pieces], rest[3 * pieces : 4 * pieces - 1]
    m_ref, held, right, sems = rest[4 * pieces - 1 :]
    here = lax.axis_index("tm")
    width = pay[0].shape[1]
    matrix = pltpu.make_async_copy(m_hbm.at[:, 0, :], m_ref, sems.at[0])
    matrix.start()
    reads = [
        pltpu.make_async_copy(columns_of(source, width, i), held.at[k * pieces + i], sems.at[1 + k * pieces + i])
        for k, source in enumerate((s1_hbm, s2_hbm, gain_hbm))
        for i in range(pieces)
    ]
    writes = [
        pltpu.make_async_copy(held.at[n], target, sems.at[1 + 3 * pieces + n])
        for n, target in enumerate(cut)
    ]
    for copy in reads:
        copy.start()
    matrix.wait()
    stack_left(back, m_ref[...].T)
    stack_left(ahead, m_ref[...])
    for read, write in zip(reads, writes):
        read.wait()
        write.start()

    @pl.when(here == 0)
    def _():
        for i in range(1, pieces):
            pay[i - 1][...] = held[i]

    @pl.when(here == depth - 1)
    def _():
        for i in range(1, pieces):
            stack_right(right, held[2 * pieces + i] * held[pieces + i])
            pay[i - 1][...] = dot(back[...], right[...])

    for write in writes:
        write.wait()


def hop_kernel(stage, depth, at, parts, after, behind, s1_ref, s2_ref, gain_ref, in_ref, ahead_ref, back_ref, *rest):
    edge, pays, (keep_ref, right) = rest[: -parts - 2], rest[-parts - 2 : -2], rest[-2:]
    here = lax.axis_index("tm")
    columns = slice(at, at + in_ref.shape[1])
    width = pays[0].shape[1]

    def send(values):
        for k, pay in enumerate(pays):
            pay[...] = values[:, k * width : (k + 1) * width]

    if edge:
        @pl.when((here == 0) | (here == depth - 1))
        def _():
            send(edge[0][:, columns] if edge[0].shape != in_ref.shape else edge[0][...])

    @pl.when(here == stage)
    def _():
        stack_right(right, in_ref[...])
        state = s1_ref[:, columns] + gain_ref[:, columns] * dot(ahead_ref[...], right[...])
        send(state)
        keep_ref[...] = state

    @pl.when(here == depth - 1 - stage)
    def _():
        swept = s2_ref[:, columns] + in_ref[...]
        keep_ref[...] = swept
        stack_right(right, gain_ref[:, columns] * swept)
        send(dot(back_ref[...], right[...]))


def last_kernel(piece, depth, regions, counts, aliased, final, after, behind, owner_ref, ahead_ref, g_ref, s1_ref, s2_ref, gain_ref, *refs):
    groups = []
    for count in counts:
        groups.append(refs[:count])
        refs = refs[count:]
    *kept, inbox = groups
    before, refs = refs[: 2 * aliased], refs[4 * aliased :]
    f_out, g_out, state, total, right, slots, sems = refs
    here = lax.axis_index("tm")
    size, width = total.shape
    resident = slots.shape[0] == 1

    def copy(source, target, which):
        return pltpu.make_async_copy(source, target, sems.at[which])

    def fetch(which):
        slot = lax.rem(which, 2)
        return copy(g_ref.at[which], slots.at[slot], 2 + slot)

    if not resident:
        fetch(0).start()
    writes = [
        copy(source, columns_of(target, width, piece - 1), 4 + k)
        for k, (source, target) in enumerate(zip(before, (f_out, g_out)))
    ]
    for write in writes:
        write.start()

    def lay(target, sources):
        part = width // len(sources)
        for k, source in enumerate(sources):
            target[:, k * part : (k + 1) * part] = source[...]

    @pl.when(here == 0)
    def _():
        lay(total, inbox)
        state[...] = s1_ref[...]
        total[...] += s2_ref[...]

    for stage in range(1, depth - 1):
        @pl.when(here == stage)
        def _():
            lay(state, kept[stage - 1])
            lay(total, kept[depth - 2 - stage])

    @pl.when(here == depth - 1)
    def _():
        lay(total, inbox)
        stack_right(right, total[...])
        state[...] = s1_ref[...] + gain_ref[...] * dot(ahead_ref[...], right[...])
        total[...] = s2_ref[...]

    if final:
        kept_state = copy(state, columns_of(f_out, width, piece), 0)
        kept_state.start()
    stack_right(right, state[...])
    owners = owner_ref[:, piece * width : (piece + 1) * width]

    def one_owner(owner, carry):
        if resident:
            g = g_ref.at[owner]
        else:
            @pl.when(owner + 1 < regions)
            def _():
                fetch(owner + 1).start()

            fetch(owner).wait()
            g = slots.at[lax.rem(owner, 2)]
        seen = dot(g[...], right[...])
        total[...] += jnp.where(owners == owner, seen, 0.0)
        return carry

    lax.fori_loop(0, regions, one_owner, 0)
    if final:
        load([copy(total, columns_of(g_out, width, piece), 1)])
        kept_state.wait()
    for write in writes:
        write.wait()


def body(search_one, search_two, column_gain, model_matrix, obs_owner, observe_matrix, error_weight, channel_mask):
    depth = lax.axis_size("tm")
    regions = lax.axis_size("region")
    size, columns = search_one.shape[1:]
    channels = observe_matrix.shape[3]
    s1, s2, gain = (far(x.reshape(size, 1, columns)) for x in (search_one, search_two, column_gain))
    matrix = far(model_matrix.reshape(size, 1, size))
    observe = far(observe_matrix.reshape(size, 1, channels))
    pieces = 4
    width = columns // pieces
    deep = stacked(size)
    top = depth - 1
    held = pltpu.VMEM((size, width), F32)
    ones = size * width

    def sent(x, *hops):
        return lax.ppermute(x, "tm", list(hops))

    square = pltpu.VMEM((size, deep), BF16)
    pay = [
        pl.pallas_call(
            functools.partial(first_kernel, depth),
            out_shape=held,
            in_specs=[HBM] * 4,
            out_specs=WHOLE,
            scratch_shapes=[
                square,
                pltpu.VMEM((size, size), F32),
                held,
                held,
                pltpu.VMEM((deep, width), BF16),
                pltpu.SemaphoreType.DMA((3,)),
            ],
            compiler_params=params(10),
            cost_estimate=cost(6 * size * ones, 24 * ones),
            name="first",
        )(s1, s2, gain, matrix)
    ]

    def rest_of(after):
        return pl.pallas_call(
            functools.partial(rest_kernel, pieces, depth),
            out_shape=[square] * 2 + ([held] + [pltpu.HBM((size, width), F32)] * (pieces - 1)) * 3 + [held] * (pieces - 1),
            in_specs=[ANY] + [HBM] * 4,
            out_specs=[WHOLE] * 2 + ([WHOLE] + [HBM] * (pieces - 1)) * 3 + [WHOLE] * (pieces - 1),
            scratch_shapes=[
                pltpu.VMEM((size, size), F32),
                pltpu.VMEM((3 * pieces, size, width), F32),
                pltpu.VMEM((deep, width), BF16),
                pltpu.SemaphoreType.DMA((6 * pieces + 1,)),
            ],
            compiler_params=params(16),
            cost_estimate=cost(6 * size * ones, 24 * ones),
            name="rest",
        )(after, s1, s2, gain, matrix)

    half, rows = packing(size)[0], packing(size)[-1]
    resident = regions % 2 == 0 and regions * size * 2 * deep <= 20 * 1024 * 1024
    def own_operator(after):
        return pl.pallas_call(
            operator_kernel,
            out_shape=pltpu.HBM((regions // 2, rows, 2 * half) if resident else (rows, 2 * half), F32),
            in_specs=[ANY] + [HBM] * 3,
            out_specs=HBM,
            scratch_shapes=[
                pltpu.VMEM((rows, 2 * half), F32),
                pltpu.VMEM((size, channels), F32),
                pltpu.VMEM((1, channels), F32),
                pltpu.VMEM((1, channels), jnp.int32),
                pltpu.VMEM((size, 3 * channels), BF16),
                pltpu.VMEM((size, 3 * channels), BF16),
                pltpu.VMEM((size, size), F32),
                pltpu.SemaphoreType.DMA((max(3, regions // 2),)),
            ],
            compiler_params=params(18),
            cost_estimate=cost(6 * size * size * channels, 8 * size * channels),
            name="operator",
        )(after, observe, far(error_weight[0]), far(channel_mask[0]))

    packed = own_operator(pay[0])
    others = rest_of(far(packed))
    ahead, back, *others = others
    s1s, s2s, gains = ([near(x) for x in others[k * pieces : (k + 1) * pieces]] for k in range(3))
    pay = [*pay, *others[3 * pieces :]]
    ahead, back = near(ahead), near(back)
    length = regions // 2
    turn = pltpu.VMEM((4 * half + 4 * up(size - 2 * half, 16), half), BF16)
    unit = pltpu.VMEM((half, half), BF16)
    shape = (regions, size, deep)

    def unpack(after, blocks, before=None):
        other = before is not None
        return pl.pallas_call(
            functools.partial(unpack_kernel, int(other), size),
            out_shape=[pltpu.VMEM(shape, BF16)] + ([] if other else [pltpu.HBM(blocks.shape, F32)]),
            in_specs=[ANY, HBM] + [WHOLE] * other,
            out_specs=[WHOLE] + ([] if other else [HBM]),
            scratch_shapes=[
                pltpu.VMEM((length, rows, 2 * half), F32),
                turn,
                unit,
                pltpu.SemaphoreType.DMA((length,)),
            ],
            input_output_aliases={2: 0} if other else {1: 1},
            compiler_params=params(8),
            cost_estimate=cost(0, size),
            name="unpack",
        )(after, far(blocks), *([near(before)] if other else []))

    def unpack_all(after):
        return pl.pallas_call(
            functools.partial(unpack_all_kernel, regions),
            out_shape=pltpu.HBM(shape, BF16),
            in_specs=[ANY, HBM],
            out_specs=HBM,
            scratch_shapes=[
                pltpu.VMEM((2, rows, 2 * half), F32),
                turn,
                unit,
                pltpu.VMEM(shape[1:], BF16),
                pltpu.SemaphoreType.DMA((3,)),
            ],
            compiler_params=params(24),
            cost_estimate=cost(0, regions * size * size * 8),
            name="unpack",
        )(after, far(gathered))

    def hop(after, behind, stage, i, came, at=0, parts=1, *edge, weight=180):
        taken = came.shape[1]
        shape = (size, taken // parts)
        return pl.pallas_call(
            functools.partial(hop_kernel, stage, depth, at, parts),
            out_shape=[pltpu.VMEM(shape, F32)] * parts + [pltpu.VMEM((size, taken), F32)],
            in_specs=[ANY] * 2 + [WHOLE] * (6 + len(edge)),
            out_specs=[WHOLE] * (parts + 1),
            scratch_shapes=[pltpu.VMEM((deep, taken), BF16)],
            compiler_params=params(8),
            cost_estimate=cost(weight * size * size * taken, 24 * size * taken),
            name="hop",
        )(after, behind, s1s[i], s2s[i], gains[i], near(came), ahead, back, *map(near, edge))

    def last(after, behind, i, done):
        groups = [store[stage, i] for stage in range(1, top)] + [[near(x) for x in inbox[i]]]
        operands = [after, behind, obs_owner, ahead, near(operators) if resident else operators, s1s[i], s2s[i], gains[i], *sum(groups, [])]
        specs = [ANY] * 2 + [WHOLE] * (len(operands) - 2)
        if not resident:
            specs[4] = HBM
        aliases = {}
        if done is not None:
            operands += [near(x) for x in done[2:]]
            aliases = {len(operands): 0, len(operands) + 1: 1}
            operands += list(done[:2])
            specs += [WHOLE] * 2 + [HBM] * 2
        final = i == pieces - 1
        slots = (1, 16, LANES) if resident else (2, size, deep)
        return pl.pallas_call(
            functools.partial(last_kernel, i, depth, regions, [len(g) for g in groups], done is not None, final),
            out_shape=[pltpu.HBM((size, 1, columns), F32)] * 2 + ([] if final else [held] * 2),
            in_specs=specs,
            out_specs=[HBM] * 2 + ([] if final else [WHOLE] * 2),
            scratch_shapes=([held] * 2 if final else [])
            + [
                pltpu.VMEM((deep, width), BF16),
                pltpu.VMEM(slots, BF16),
                pltpu.SemaphoreType.DMA((6,)),
            ],
            input_output_aliases=aliases,
            compiler_params=params(8 if resident else 24),
            cost_estimate=cost(size * ones, size * ones),
            name="last",
        )(*operands)

    def link(low, by=1):
        high = top - low
        return [(low, low + by), (high, high - by)]

    both = link(0) + link(2)
    narrow = width // 2
    store, inbox = {}, {i: [] for i in range(pieces)}

    def keep(stage, i, part):
        store.setdefault((stage, i), []).append(near(part))

    def q(after, i, behind=None):
        out, kept = hop(after, after if behind is None else behind, 1, i, arrived[i])
        keep(1, i, kept)
        return sent(out, *link(1, 1 if i < 2 else 2)), kept

    arrived = [sent(pay[i], *link(0)) for i in range(pieces)]
    middle = [None] * pieces
    if resident:
        kinds = [list(range(kind, regions, 2)) for kind in range(2)]
        alike = lax.all_to_all(packed, "region", 0, 0, axis_index_groups=kinds)
    else:
        gathered = lax.all_gather(packed, "region")

    middle[0], after = q(ahead, 0)
    middle[1], after = q(after, 1)
    out, after = hop(after, after, 2, 0, middle[0])
    keep(2, 0, after)
    inbox[0].append(sent(out, *link(2)))
    middle[2], after = q(after, 2)
    middle[3], after = q(after, 3)
    *outs, after = hop(after, inbox[0][0], 2, 1, middle[1], 0, 2, middle[2])
    keep(2, 1, after)
    turned = [sent(out, *both) for out in outs]
    inbox[1] += turned
    follow = []

    def r2(after, k):
        out, after = hop(after, after, 2, 2, turned[k], k * narrow, 1, middle[3], weight=6)
        keep(2, 2, after)
        follow.append(sent(out, *both))
        return near(after)

    def r3(after, k):
        out, after = hop(after, after, 2, 3, follow[k], k * narrow, weight=6)
        keep(2, 3, after)
        inbox[3].append(sent(out, *link(2)))
        return near(after)

    after = r2(r2(near(after), 0), 1)
    inbox[2] += follow
    if resident:
        operators, alike = unpack(after, alike)
        others = lax.ppermute(far(alike), "region", [(r, r ^ 1) for r in range(regions)])
        operators = near(unpack(after, others, operators)[0])
        after = r3(operators, 0)
    else:
        after = r3(after, 0)
        operators = far(unpack_all(after))
    done = last(after, after, 0, None)
    after = r3(done[3], 1)
    done = last(after, after, 1, done)
    done = last(done[3], inbox[3][0], 2, done)
    done = last(done[3], done[3], 3, done)[:2]
    return tuple(x.reshape(1, size, columns) for x in done)


def solution(mesh):
    return jax.shard_map(
        body,
        mesh=mesh,
        in_specs=(
            P("tm", None, "region"),
            P("tm", None, "region"),
            P("tm", None, "region"),
            P("tm", None, None),
            P("tm", "region"),
            P("tm", "region", None, None),
            P("tm", "region", None),
            P("tm", "region", None),
        ),
        out_specs=(P("tm", None, "region"), P("tm", None, "region")),
        check_vma=False,
    )
```

```python
import functools

import jax
import jax.numpy as jnp
from jax import lax
from jax.experimental import pallas as pl
from jax.experimental.pallas import tpu as pltpu
from jax.sharding import PartitionSpec as P

LANES = 128
F32 = jnp.float32
BF16 = jnp.bfloat16
WHOLE = pl.BlockSpec(memory_space=pltpu.VMEM)
ANY = pl.BlockSpec(memory_space=pl.ANY)
HBM = pl.BlockSpec(memory_space=pltpu.HBM)


def far(x):
    return pltpu.with_memory_space_constraint(x, pltpu.HBM)


def near(x):
    return pltpu.with_memory_space_constraint(x, pltpu.VMEM)


def params(mebibytes):
    return pltpu.CompilerParams(vmem_limit_bytes=mebibytes * 1024 * 1024)


def cost(flops, touched):
    return pl.CostEstimate(flops=int(flops), bytes_accessed=int(touched), transcendentals=0)


def up(size, to):
    return -(-size // to) * to


def split(x):
    high = x.astype(BF16)
    return high, (x - high.astype(F32)).astype(BF16)


def dot(left, right):
    return jnp.dot(left, right, preferred_element_type=F32)


def stacking(size):
    main = size // LANES * LANES
    rest = size - main
    return main, rest, up(rest, 16)


def stacked(size):
    main, _, room = stacking(size)
    return 3 * (main + room)


def stack_left(ref, matrix):
    main, rest, room = stacking(matrix.shape[1])
    if room > rest:
        ref[:, 3 * main :] = jnp.zeros((matrix.shape[0], 3 * room), BF16)
    for k, term in enumerate(split(matrix)):
        for at in (0, 1) if k == 0 else (2,):
            ref[:, at * main : (at + 1) * main] = term[:, 0:main]
            if rest:
                start = 3 * main + at * room
                ref[:, start : start + rest] = term[:, main : main + rest]


def stack_right(ref, x):
    main, rest, room = stacking(x.shape[0])
    for k, term in enumerate(split(x)):
        end = term[main : main + rest, :]
        if room > rest:
            end = jnp.concatenate([end, jnp.zeros((room - rest, x.shape[1]), BF16)], axis=0)
        for at in (0, 2) if k == 0 else (1,):
            ref[at * main : (at + 1) * main, :] = term[0:main, :]
            if rest:
                start = 3 * main + at * room
                ref[start : start + room, :] = end


def columns_of(source, width, piece):
    return source.at[:, 0, piece * width : (piece + 1) * width]


def load(copies):
    for copy in copies:
        copy.start()
    for copy in copies:
        copy.wait()


def packing(size):
    half = size // (2 * LANES) * LANES
    rest = size - 2 * half
    cell = LANES // 2 if rest <= LANES // 2 else LANES
    across = 2 * half // cell
    strip = half
    corner = strip + up(rest + 1, 8)
    height = corner + 8 * (up(up(rest, 8) // 8, across) // across)
    cells = [
        (8 * g, min(8, rest - 8 * g), corner + 8 * (g // across), cell * (g % across))
        for g in range(up(rest, 8) // 8)
    ]
    return half, rest, cells, strip, strip + rest, height


def operator_kernel(after, h_hbm, w_hbm, m_hbm, copies_hbm, out_ref, h_ref, w_ref, m_ref, left, right, full, sems):
    size, channels = h_ref.shape
    half, rest, cells, strip, diagonal, _ = packing(size)
    load(
        [
            pltpu.make_async_copy(h_hbm.at[:, 0, :], h_ref, sems.at[0]),
            pltpu.make_async_copy(w_hbm, w_ref, sems.at[1]),
            pltpu.make_async_copy(m_hbm, m_ref, sems.at[2]),
        ]
    )
    h = h_ref[...]
    high, low = split(h * (w_ref[...] * m_ref[...].astype(F32)))
    left[:, 0:channels] = high
    left[:, channels : 2 * channels] = high
    left[:, 2 * channels : 3 * channels] = low
    high, low = split(h)
    right[:, 0:channels] = high
    right[:, channels : 2 * channels] = low
    right[:, 2 * channels : 3 * channels] = high
    full[...] = lax.dot_general(
        left[...], right[...], (((1,), (1,)), ((), ())), preferred_element_type=F32
    )
    first = full[0:half, 0:half]
    second = full[half : 2 * half, half : 2 * half]
    row = lax.broadcasted_iota(jnp.int32, (half, half), 0)
    col = lax.broadcasted_iota(jnp.int32, (half, half), 1)
    out_ref[strip:, :] = jnp.zeros((out_ref.shape[0] - strip, out_ref.shape[1]), F32)
    out_ref[0:half, 0:half] = jnp.where(row <= col, first, second)
    out_ref[0:half, half : 2 * half] = full[0:half, half : 2 * half]
    out_ref[strip : strip + rest, :] = full[2 * half : size, 0 : 2 * half]
    for row_at, take, at, lane in cells:
        out_ref[at : at + take, lane : lane + rest] = full[
            2 * half + row_at : 2 * half + row_at + take, 2 * half : size
        ]
    out_ref[diagonal : diagonal + 1, 0:half] = jnp.sum(
        jnp.where(row == col, second, 0.0), axis=0, keepdims=True
    )
    if len(copies_hbm.shape) == 2:
        load([pltpu.make_async_copy(out_ref, copies_hbm, sems.at[0])])
    else:
        load([pltpu.make_async_copy(out_ref, copies_hbm.at[k], sems.at[k]) for k in range(copies_hbm.shape[0])])


def make_unit(unit, turn):
    row = lax.broadcasted_iota(jnp.int32, unit.shape, 0)
    col = lax.broadcasted_iota(jnp.int32, unit.shape, 1)
    unit[...] = jnp.where(row == col, 1.0, 0.0).astype(BF16)
    turn[...] = jnp.zeros(turn.shape, BF16)


def unpack_kernel(other, size, after, *refs):
    slots, turn, unit, sems = refs[-4:]
    pairs = slots.shape[0]
    blocks, out_ref = (refs[:pairs], refs[pairs + 1]) if other else ([refs[0].at[k] for k in range(pairs)], refs[1])
    kind = lax.rem(lax.axis_index("region") + other, 2)
    fetches = [pltpu.make_async_copy(blocks[k], slots.at[k], sems.at[k]) for k in range(pairs)]
    passes = [pltpu.make_async_copy(slots.at[k], refs[2 + k], sems.at[pairs + k]) for k in range(pairs * (1 - other))]
    for fetch in fetches:
        fetch.start()
    make_unit(unit, turn)
    for fetch in fetches:
        fetch.wait()
    for passing in passes:
        passing.start()

    def one_block(k, carry):
        unfold(size, slots.at[k], out_ref.at[2 * k + kind], turn, unit)
        return carry

    lax.fori_loop(0, pairs, one_block, 0)
    for passing in passes:
        passing.wait()


def unpack_all_kernel(regions, after, packed_hbm, out_hbm, slots, turn, unit, stacks, sems):
    make_unit(unit, turn)

    def fetch(which):
        slot = lax.rem(which, 2)
        return pltpu.make_async_copy(packed_hbm.at[which], slots.at[slot], sems.at[slot])

    def one_owner(owner, carry):
        @pl.when(owner + 1 < regions)
        def _():
            fetch(owner + 1).start()

        fetch(owner).wait()
        unfold(stacks.shape[0], slots.at[lax.rem(owner, 2)], stacks, turn, unit)
        load([pltpu.make_async_copy(stacks, out_hbm.at[owner], sems.at[2])])
        return carry

    fetch(0).start()
    lax.fori_loop(0, regions, one_owner, 0)


def unfold(size, packed_ref, out_ref, turn, unit):
    half, rest, cells, strip, diagonal, _ = packing(size)
    main, over, room = stacking(size)
    gap = up(rest, 16)
    square = split(packed_ref[0:half, 0:half])
    side = split(packed_ref[0:half, half : 2 * half])
    stripe = split(packed_ref[strip : strip + rest, :])
    for k in range(2):
        turn[k * half : (k + 1) * half, :] = square[k]
        turn[(2 + k) * half : (3 + k) * half, :] = side[k]
        for j in range(2):
            at = 4 * half + (2 * k + j) * gap
            turn[at : at + rest, :] = stripe[k][:, j * half : (j + 1) * half]
    turned = lax.dot_general(
        unit[...], turn[...], (((1,), (1,)), ((), ())), preferred_element_type=F32
    )
    row = lax.broadcasted_iota(jnp.int32, (half, half), 0)
    col = lax.broadcasted_iota(jnp.int32, (half, half), 1)
    ends = split(packed_ref[diagonal : diagonal + 1, 0:half])
    if room > over:
        out_ref[:, 3 * main :] = jnp.zeros((size, 3 * room), BF16)

    def put(k, rows, columns, value):
        for at in (0, 1) if k == 0 else (2,):
            if columns < main:
                out_ref[rows : rows + value.shape[0], at * main + columns : at * main + columns + value.shape[1]] = value
            else:
                start = 3 * main + at * room
                out_ref[rows : rows + value.shape[0], start : start + value.shape[1]] = value

    for k in range(2):
        here = square[k].astype(F32)
        there = turned[:, k * half : (k + 1) * half]
        put(k, 0, 0, jnp.where(row <= col, here, there).astype(BF16))
        end = jnp.broadcast_to(ends[k].astype(F32), (half, half))
        put(k, half, half, jnp.where(row > col, here, jnp.where(row == col, end, there)).astype(BF16))
        put(k, 0, half, side[k])
        put(k, half, 0, turned[:, (2 + k) * half : (3 + k) * half].astype(BF16))
        put(k, 2 * half, 0, stripe[k])
        for j in range(2):
            at = 4 * half + (2 * k + j) * gap
            put(k, j * half, 2 * half, turned[:, at : at + rest].astype(BF16))
    for row_at, take, at, lane in cells:
        corner = split(packed_ref[at : at + take, lane : lane + rest])
        for k in range(2):
            put(k, 2 * half + row_at, 2 * half, corner[k])


def first_kernel(depth, s1_hbm, s2_hbm, gain_hbm, m_hbm, pay, back, m_ref, s2, gain, right, sems):
    here = lax.axis_index("tm")
    width = pay.shape[1]

    @pl.when(here == 0)
    def _():
        load([pltpu.make_async_copy(columns_of(s1_hbm, width, 0), pay, sems.at[0])])

    @pl.when(here == depth - 1)
    def _():
        load(
            [
                pltpu.make_async_copy(m_hbm.at[:, 0, :], m_ref, sems.at[0]),
                pltpu.make_async_copy(columns_of(s2_hbm, width, 0), s2, sems.at[1]),
                pltpu.make_async_copy(columns_of(gain_hbm, width, 0), gain, sems.at[2]),
            ]
        )
        stack_left(back, m_ref[...].T)
        stack_right(right, gain[...] * s2[...])
        pay[...] = dot(back[...], right[...])


def rest_kernel(pieces, depth, after, s1_hbm, s2_hbm, gain_hbm, m_hbm, ahead, back, *rest):
    cut, pay = rest[: 3 * pieces], rest[3 * pieces : 4 * pieces - 1]
    m_ref, held, right, sems = rest[4 * pieces - 1 :]
    here = lax.axis_index("tm")
    width = pay[0].shape[1]
    matrix = pltpu.make_async_copy(m_hbm.at[:, 0, :], m_ref, sems.at[0])
    matrix.start()
    reads = [
        pltpu.make_async_copy(columns_of(source, width, i), held.at[k * pieces + i], sems.at[1 + k * pieces + i])
        for k, source in enumerate((s1_hbm, s2_hbm, gain_hbm))
        for i in range(pieces)
    ]
    writes = [
        pltpu.make_async_copy(held.at[n], target, sems.at[1 + 3 * pieces + n])
        for n, target in enumerate(cut)
    ]
    for copy in reads:
        copy.start()
    matrix.wait()
    stack_left(back, m_ref[...].T)
    stack_left(ahead, m_ref[...])
    for read, write in zip(reads, writes):
        read.wait()
        write.start()

    @pl.when(here == 0)
    def _():
        for i in range(1, pieces):
            pay[i - 1][...] = held[i]

    @pl.when(here == depth - 1)
    def _():
        for i in range(1, pieces):
            stack_right(right, held[2 * pieces + i] * held[pieces + i])
            pay[i - 1][...] = dot(back[...], right[...])

    for write in writes:
        write.wait()


def hop_kernel(stage, depth, at, parts, after, behind, s1_ref, s2_ref, gain_ref, in_ref, ahead_ref, back_ref, *rest):
    edge, pays, (keep_ref, right) = rest[: -parts - 2], rest[-parts - 2 : -2], rest[-2:]
    here = lax.axis_index("tm")
    columns = slice(at, at + in_ref.shape[1])
    width = pays[0].shape[1]

    def send(values):
        for k, pay in enumerate(pays):
            pay[...] = values[:, k * width : (k + 1) * width]

    @pl.when((here == 0) | (here == depth - 1))
    def _():
        keep_ref[...] = in_ref[...]
        if edge:
            send(edge[0][:, columns] if edge[0].shape != in_ref.shape else edge[0][...])

    @pl.when(here == stage)
    def _():
        stack_right(right, in_ref[...])
        state = s1_ref[:, columns] + gain_ref[:, columns] * dot(ahead_ref[...], right[...])
        send(state)
        keep_ref[...] = state

    @pl.when(here == depth - 1 - stage)
    def _():
        swept = s2_ref[:, columns] + in_ref[...]
        keep_ref[...] = swept
        stack_right(right, gain_ref[:, columns] * swept)
        send(dot(back_ref[...], right[...]))


def last_kernel(piece, depth, regions, counts, aliased, final, after, behind, owner_ref, ahead_ref, g_ref, s1_ref, s2_ref, gain_ref, *refs):
    groups = []
    for count in counts:
        groups.append(refs[:count])
        refs = refs[count:]
    *kept, inbox = groups
    before, refs = refs[: 2 * aliased], refs[4 * aliased :]
    f_out, g_out, state, total, right, slots, sems = refs
    here = lax.axis_index("tm")
    size, width = total.shape
    resident = slots.shape[0] == 1

    def copy(source, target, which):
        return pltpu.make_async_copy(source, target, sems.at[which])

    def fetch(which):
        slot = lax.rem(which, 2)
        return copy(g_ref.at[which], slots.at[slot], 2 + slot)

    if not resident:
        fetch(0).start()
    writes = [
        copy(source, columns_of(target, width, piece - 1), 4 + k)
        for k, (source, target) in enumerate(zip(before, (f_out, g_out)))
    ]
    for write in writes:
        write.start()

    def lay(target, sources):
        part = width // len(sources)
        for k, source in enumerate(sources):
            target[:, k * part : (k + 1) * part] = source[...]

    @pl.when(here == 0)
    def _():
        lay(total, inbox)
        state[...] = s1_ref[...]
        total[...] += s2_ref[...]

    for stage in range(1, depth - 1):
        @pl.when(here == stage)
        def _():
            lay(state, kept[stage - 1])
            lay(total, kept[depth - 2 - stage])

    @pl.when(here == depth - 1)
    def _():
        lay(total, inbox)
        stack_right(right, total[...])
        state[...] = s1_ref[...] + gain_ref[...] * dot(ahead_ref[...], right[...])
        total[...] = s2_ref[...]

    if final:
        kept_state = copy(state, columns_of(f_out, width, piece), 0)
        kept_state.start()
    stack_right(right, state[...])
    owners = owner_ref[:, piece * width : (piece + 1) * width]

    def one_owner(owner, carry):
        if resident:
            g = g_ref.at[owner]
        else:
            @pl.when(owner + 1 < regions)
            def _():
                fetch(owner + 1).start()

            fetch(owner).wait()
            g = slots.at[lax.rem(owner, 2)]
        seen = dot(g[...], right[...])
        total[...] += jnp.where(owners == owner, seen, 0.0)
        return carry

    lax.fori_loop(0, regions, one_owner, 0)
    if final:
        load([copy(total, columns_of(g_out, width, piece), 1)])
        kept_state.wait()
    for write in writes:
        write.wait()


def body(search_one, search_two, column_gain, model_matrix, obs_owner, observe_matrix, error_weight, channel_mask):
    depth = lax.axis_size("tm")
    regions = lax.axis_size("region")
    size, columns = search_one.shape[1:]
    channels = observe_matrix.shape[3]
    s1, s2, gain = (far(x.reshape(size, 1, columns)) for x in (search_one, search_two, column_gain))
    matrix = far(model_matrix.reshape(size, 1, size))
    observe = far(observe_matrix.reshape(size, 1, channels))
    pieces = 4
    width = columns // pieces
    deep = stacked(size)
    top = depth - 1
    held = pltpu.VMEM((size, width), F32)
    ones = size * width

    def sent(x, *hops):
        return lax.ppermute(x, "tm", list(hops))

    square = pltpu.VMEM((size, deep), BF16)
    pay = [
        pl.pallas_call(
            functools.partial(first_kernel, depth),
            out_shape=held,
            in_specs=[HBM] * 4,
            out_specs=WHOLE,
            scratch_shapes=[
                square,
                pltpu.VMEM((size, size), F32),
                held,
                held,
                pltpu.VMEM((deep, width), BF16),
                pltpu.SemaphoreType.DMA((3,)),
            ],
            compiler_params=params(10),
            cost_estimate=cost(6 * size * ones, 24 * ones),
            name="first",
        )(s1, s2, gain, matrix)
    ]

    def rest_of(after):
        return pl.pallas_call(
            functools.partial(rest_kernel, pieces, depth),
            out_shape=[square] * 2 + ([held] + [pltpu.HBM((size, width), F32)] * (pieces - 1)) * 3 + [held] * (pieces - 1),
            in_specs=[ANY] + [HBM] * 4,
            out_specs=[WHOLE] * 2 + ([WHOLE] + [HBM] * (pieces - 1)) * 3 + [WHOLE] * (pieces - 1),
            scratch_shapes=[
                pltpu.VMEM((size, size), F32),
                pltpu.VMEM((3 * pieces, size, width), F32),
                pltpu.VMEM((deep, width), BF16),
                pltpu.SemaphoreType.DMA((6 * pieces + 1,)),
            ],
            compiler_params=params(16),
            cost_estimate=cost(6 * size * ones, 24 * ones),
            name="rest",
        )(after, s1, s2, gain, matrix)

    half, rows = packing(size)[0], packing(size)[-1]
    resident = regions % 2 == 0 and regions * size * 2 * deep <= 20 * 1024 * 1024
    def own_operator(after):
        return pl.pallas_call(
            operator_kernel,
            out_shape=pltpu.HBM((regions // 2, rows, 2 * half) if resident else (rows, 2 * half), F32),
            in_specs=[ANY] + [HBM] * 3,
            out_specs=HBM,
            scratch_shapes=[
                pltpu.VMEM((rows, 2 * half), F32),
                pltpu.VMEM((size, channels), F32),
                pltpu.VMEM((1, channels), F32),
                pltpu.VMEM((1, channels), jnp.int32),
                pltpu.VMEM((size, 3 * channels), BF16),
                pltpu.VMEM((size, 3 * channels), BF16),
                pltpu.VMEM((size, size), F32),
                pltpu.SemaphoreType.DMA((max(3, regions // 2),)),
            ],
            compiler_params=params(18),
            cost_estimate=cost(6 * size * size * channels, 8 * size * channels),
            name="operator",
        )(after, observe, far(error_weight[0]), far(channel_mask[0]))

    packed = own_operator(pay[0])
    others = rest_of(far(packed))
    ahead, back, *others = others
    s1s, s2s, gains = ([near(x) for x in others[k * pieces : (k + 1) * pieces]] for k in range(3))
    pay = [*pay, *others[3 * pieces :]]
    ahead, back = near(ahead), near(back)
    length = regions // 2
    turn = pltpu.VMEM((4 * half + 4 * up(size - 2 * half, 16), half), BF16)
    unit = pltpu.VMEM((half, half), BF16)
    shape = (regions, size, deep)

    def unpack(after, blocks, before=None):
        other = before is not None
        return pl.pallas_call(
            functools.partial(unpack_kernel, int(other), size),
            out_shape=[pltpu.VMEM(shape, BF16)] + [pltpu.HBM((rows, 2 * half), F32)] * (length * (not other)),
            in_specs=[ANY] + [HBM] * len(blocks) + [WHOLE] * other,
            out_specs=[WHOLE] + [HBM] * (length * (not other)),
            scratch_shapes=[
                pltpu.VMEM((length, rows, 2 * half), F32),
                turn,
                unit,
                pltpu.SemaphoreType.DMA((2 * length,)),
            ],
            input_output_aliases={1 + len(blocks): 0} if other else {},
            compiler_params=params(8),
            cost_estimate=cost(0, size),
            name="unpack",
        )(after, *map(far, blocks), *([near(before)] if other else []))

    def unpack_all(after):
        return pl.pallas_call(
            functools.partial(unpack_all_kernel, regions),
            out_shape=pltpu.HBM(shape, BF16),
            in_specs=[ANY, HBM],
            out_specs=HBM,
            scratch_shapes=[
                pltpu.VMEM((2, rows, 2 * half), F32),
                turn,
                unit,
                pltpu.VMEM(shape[1:], BF16),
                pltpu.SemaphoreType.DMA((3,)),
            ],
            compiler_params=params(24),
            cost_estimate=cost(0, regions * size * size * 8),
            name="unpack",
        )(after, far(gathered))

    def hop(after, behind, stage, i, came, at=0, parts=1, *edge, weight=180):
        taken = came.shape[1]
        shape = (size, taken // parts)
        return pl.pallas_call(
            functools.partial(hop_kernel, stage, depth, at, parts),
            out_shape=[pltpu.VMEM(shape, F32)] * parts + [pltpu.VMEM((size, taken), F32)],
            in_specs=[ANY] * 2 + [WHOLE] * (6 + len(edge)),
            out_specs=[WHOLE] * (parts + 1),
            scratch_shapes=[pltpu.VMEM((deep, taken), BF16)],
            compiler_params=params(8),
            cost_estimate=cost(weight * size * size * taken, 24 * size * taken),
            name="hop",
        )(after, behind, s1s[i], s2s[i], gains[i], near(came), ahead, back, *map(near, edge))

    def last(after, behind, i, done):
        groups = [store[stage, i] for stage in range(1, top)] + [[near(x) for x in inbox[i]]]
        operands = [after, behind, obs_owner, ahead, near(operators) if resident else operators, s1s[i], s2s[i], gains[i], *sum(groups, [])]
        specs = [ANY] * 2 + [WHOLE] * (len(operands) - 2)
        if not resident:
            specs[4] = HBM
        aliases = {}
        if done is not None:
            operands += [near(x) for x in done[2:]]
            aliases = {len(operands): 0, len(operands) + 1: 1}
            operands += list(done[:2])
            specs += [WHOLE] * 2 + [HBM] * 2
        final = i == pieces - 1
        slots = (1, 16, LANES) if resident else (2, size, deep)
        return pl.pallas_call(
            functools.partial(last_kernel, i, depth, regions, [len(g) for g in groups], done is not None, final),
            out_shape=[pltpu.HBM((size, 1, columns), F32)] * 2 + ([] if final else [held] * 2),
            in_specs=specs,
            out_specs=[HBM] * 2 + ([] if final else [WHOLE] * 2),
            scratch_shapes=([held] * 2 if final else [])
            + [
                pltpu.VMEM((deep, width), BF16),
                pltpu.VMEM(slots, BF16),
                pltpu.SemaphoreType.DMA((6,)),
            ],
            input_output_aliases=aliases,
            compiler_params=params(8 if resident else 24),
            cost_estimate=cost(size * ones, size * ones),
            name="last",
        )(*operands)

    def link(low, by=1):
        high = top - low
        return [(low, low + by), (high, high - by)]

    both = link(0) + link(2)
    narrow = width // 2
    store, inbox = {}, {i: [] for i in range(pieces)}

    def keep(stage, i, part):
        store.setdefault((stage, i), []).append(near(part))

    def q(after, i, behind=None):
        out, kept = hop(after, after if behind is None else behind, 1, i, arrived[i])
        keep(1, i, kept)
        return sent(out, *link(1, 1 if i < 2 else 2)), kept

    arrived = [sent(pay[i], *link(0)) for i in range(pieces)]
    middle = [None] * pieces
    if resident:
        kinds = [list(range(kind, regions, 2)) for kind in range(2)]
        alike = lax.all_to_all(packed, "region", 0, 0, axis_index_groups=kinds)
    else:
        gathered = lax.all_gather(packed, "region")

    middle[0], after = q(ahead, 0)
    middle[1], after = q(after, 1)
    out, after = hop(after, after, 2, 0, middle[0])
    keep(2, 0, after)
    inbox[0].append(sent(out, *link(2)))
    middle[2], after = q(after, 2)
    middle[3], after = q(after, 3)
    *outs, after = hop(after, inbox[0][0], 2, 1, middle[1], 0, 2, middle[2])
    keep(2, 1, after)
    turned = [sent(out, *both) for out in outs]
    follow = []

    def r2(after, k):
        out, after = hop(after, after, 2, 2, turned[k], k * narrow, 1, middle[3])
        keep(2, 2, after)
        follow.append(sent(out, *both))
        return near(after)

    def r3(after, k):
        out, after = hop(after, after, 2, 3, follow[k], k * narrow, weight=6)
        keep(2, 3, after)
        inbox[3].append(sent(out, *link(2)))
        return near(after)

    if resident:
        operators, *alike = unpack(near(after), [alike])
        others = [lax.ppermute(far(x), "region", [(r, r ^ 1) for r in range(regions)]) for x in alike]
        after = r2(r2(near(operators), 0), 1)
        operators = near(unpack(after, others, operators)[0])
        after = r3(operators, 0)
    else:
        after = r3(r2(r2(after, 0), 1), 0)
        operators = far(unpack_all(after))
    inbox[1] = store[2, 2]
    done = last(after, after, 0, None)
    after = r3(done[3], 1)
    done = last(after, after, 1, done)
    inbox[2] = store[2, 3]
    done = last(done[3], inbox[3][0], 2, done)
    done = last(done[3], done[3], 3, done)[:2]
    return tuple(x.reshape(1, size, columns) for x in done)


def solution(mesh):
    return jax.shard_map(
        body,
        mesh=mesh,
        in_specs=(
            P("tm", None, "region"),
            P("tm", None, "region"),
            P("tm", None, "region"),
            P("tm", None, None),
            P("tm", "region"),
            P("tm", "region", None, None),
            P("tm", "region", None),
            P("tm", "region", None),
        ),
        out_specs=(P("tm", None, "region"), P("tm", None, "region")),
        check_vma=False,
    )
```

```python
import functools

import jax
import jax.numpy as jnp
from jax import lax
from jax.experimental import pallas as pl
from jax.experimental.pallas import tpu as pltpu
from jax.sharding import PartitionSpec as P

LANES = 128
F32 = jnp.float32
BF16 = jnp.bfloat16
WHOLE = pl.BlockSpec(memory_space=pltpu.VMEM)
ANY = pl.BlockSpec(memory_space=pl.ANY)
HBM = pl.BlockSpec(memory_space=pltpu.HBM)


def far(x):
    return pltpu.with_memory_space_constraint(x, pltpu.HBM)


def near(x):
    return pltpu.with_memory_space_constraint(x, pltpu.VMEM)


def params(mebibytes):
    return pltpu.CompilerParams(vmem_limit_bytes=mebibytes * 1024 * 1024)


def cost(flops, touched):
    return pl.CostEstimate(flops=int(flops), bytes_accessed=int(touched), transcendentals=0)


def up(size, to):
    return -(-size // to) * to


def split(x):
    high = x.astype(BF16)
    return high, (x - high.astype(F32)).astype(BF16)


def dot(left, right):
    return jnp.dot(left, right, preferred_element_type=F32)


def stacking(size):
    main = size // LANES * LANES
    rest = size - main
    return main, rest, up(rest, 16)


def stacked(size):
    main, _, room = stacking(size)
    return 3 * (main + room)


def stack_left(ref, matrix):
    main, rest, room = stacking(matrix.shape[1])
    if room > rest:
        ref[:, 3 * main :] = jnp.zeros((matrix.shape[0], 3 * room), BF16)
    for k, term in enumerate(split(matrix)):
        for at in (0, 1) if k == 0 else (2,):
            ref[:, at * main : (at + 1) * main] = term[:, 0:main]
            if rest:
                start = 3 * main + at * room
                ref[:, start : start + rest] = term[:, main : main + rest]


def stack_right(ref, x):
    main, rest, room = stacking(x.shape[0])
    for k, term in enumerate(split(x)):
        end = term[main : main + rest, :]
        if room > rest:
            end = jnp.concatenate([end, jnp.zeros((room - rest, x.shape[1]), BF16)], axis=0)
        for at in (0, 2) if k == 0 else (1,):
            ref[at * main : (at + 1) * main, :] = term[0:main, :]
            if rest:
                start = 3 * main + at * room
                ref[start : start + room, :] = end


def columns_of(source, width, piece):
    return source.at[:, 0, piece * width : (piece + 1) * width]


def load(copies):
    for copy in copies:
        copy.start()
    for copy in copies:
        copy.wait()


def packing(size):
    half = size // (2 * LANES) * LANES
    rest = size - 2 * half
    cell = LANES // 2 if rest <= LANES // 2 else LANES
    across = 2 * half // cell
    strip = half
    corner = strip + up(rest + 1, 8)
    height = corner + 8 * (up(up(rest, 8) // 8, across) // across)
    cells = [
        (8 * g, min(8, rest - 8 * g), corner + 8 * (g // across), cell * (g % across))
        for g in range(up(rest, 8) // 8)
    ]
    return half, rest, cells, strip, strip + rest, height


def operator_kernel(after, h_hbm, w_hbm, m_hbm, copies_hbm, out_ref, h_ref, w_ref, m_ref, left, right, full, sems):
    size, channels = h_ref.shape
    half, rest, cells, strip, diagonal, _ = packing(size)
    load(
        [
            pltpu.make_async_copy(h_hbm.at[:, 0, :], h_ref, sems.at[0]),
            pltpu.make_async_copy(w_hbm, w_ref, sems.at[1]),
            pltpu.make_async_copy(m_hbm, m_ref, sems.at[2]),
        ]
    )
    h = h_ref[...]
    high, low = split(h * (w_ref[...] * m_ref[...].astype(F32)))
    left[:, 0:channels] = high
    left[:, channels : 2 * channels] = high
    left[:, 2 * channels : 3 * channels] = low
    high, low = split(h)
    right[:, 0:channels] = high
    right[:, channels : 2 * channels] = low
    right[:, 2 * channels : 3 * channels] = high
    full[...] = lax.dot_general(
        left[...], right[...], (((1,), (1,)), ((), ())), preferred_element_type=F32
    )
    first = full[0:half, 0:half]
    second = full[half : 2 * half, half : 2 * half]
    row = lax.broadcasted_iota(jnp.int32, (half, half), 0)
    col = lax.broadcasted_iota(jnp.int32, (half, half), 1)
    out_ref[strip:, :] = jnp.zeros((out_ref.shape[0] - strip, out_ref.shape[1]), F32)
    out_ref[0:half, 0:half] = jnp.where(row <= col, first, second)
    out_ref[0:half, half : 2 * half] = full[0:half, half : 2 * half]
    out_ref[strip : strip + rest, :] = full[2 * half : size, 0 : 2 * half]
    for row_at, take, at, lane in cells:
        out_ref[at : at + take, lane : lane + rest] = full[
            2 * half + row_at : 2 * half + row_at + take, 2 * half : size
        ]
    out_ref[diagonal : diagonal + 1, 0:half] = jnp.sum(
        jnp.where(row == col, second, 0.0), axis=0, keepdims=True
    )
    if len(copies_hbm.shape) == 2:
        load([pltpu.make_async_copy(out_ref, copies_hbm, sems.at[0])])
    else:
        load([pltpu.make_async_copy(out_ref, copies_hbm.at[k], sems.at[k]) for k in range(copies_hbm.shape[0])])


def make_unit(unit, turn):
    row = lax.broadcasted_iota(jnp.int32, unit.shape, 0)
    col = lax.broadcasted_iota(jnp.int32, unit.shape, 1)
    unit[...] = jnp.where(row == col, 1.0, 0.0).astype(BF16)
    turn[...] = jnp.zeros(turn.shape, BF16)


def unpack_kernel(other, size, after, *refs):
    slots, turn, unit, sems = refs[-4:]
    pairs = slots.shape[0]
    blocks, out_ref = (refs[:pairs], refs[pairs + 1]) if other else ([refs[0].at[k] for k in range(pairs)], refs[1])
    kind = lax.rem(lax.axis_index("region") + other, 2)
    fetches = [pltpu.make_async_copy(blocks[k], slots.at[k], sems.at[k]) for k in range(pairs)]
    passes = [pltpu.make_async_copy(slots.at[k], refs[2 + k], sems.at[pairs + k]) for k in range(pairs * (1 - other))]
    for fetch in fetches:
        fetch.start()
    make_unit(unit, turn)
    for fetch in fetches:
        fetch.wait()
    for passing in passes:
        passing.start()

    def one_block(k, carry):
        unfold(size, slots.at[k], out_ref.at[2 * k + kind], turn, unit)
        return carry

    lax.fori_loop(0, pairs, one_block, 0)
    for passing in passes:
        passing.wait()


def unpack_all_kernel(regions, after, packed_hbm, out_hbm, slots, turn, unit, stacks, sems):
    make_unit(unit, turn)

    def fetch(which):
        slot = lax.rem(which, 2)
        return pltpu.make_async_copy(packed_hbm.at[which], slots.at[slot], sems.at[slot])

    def one_owner(owner, carry):
        @pl.when(owner + 1 < regions)
        def _():
            fetch(owner + 1).start()

        fetch(owner).wait()
        unfold(stacks.shape[0], slots.at[lax.rem(owner, 2)], stacks, turn, unit)
        load([pltpu.make_async_copy(stacks, out_hbm.at[owner], sems.at[2])])
        return carry

    fetch(0).start()
    lax.fori_loop(0, regions, one_owner, 0)


def unfold(size, packed_ref, out_ref, turn, unit):
    half, rest, cells, strip, diagonal, _ = packing(size)
    main, over, room = stacking(size)
    gap = up(rest, 16)
    square = split(packed_ref[0:half, 0:half])
    side = split(packed_ref[0:half, half : 2 * half])
    stripe = split(packed_ref[strip : strip + rest, :])
    for k in range(2):
        turn[k * half : (k + 1) * half, :] = square[k]
        turn[(2 + k) * half : (3 + k) * half, :] = side[k]
        for j in range(2):
            at = 4 * half + (2 * k + j) * gap
            turn[at : at + rest, :] = stripe[k][:, j * half : (j + 1) * half]
    turned = lax.dot_general(
        unit[...], turn[...], (((1,), (1,)), ((), ())), preferred_element_type=F32
    )
    row = lax.broadcasted_iota(jnp.int32, (half, half), 0)
    col = lax.broadcasted_iota(jnp.int32, (half, half), 1)
    ends = split(packed_ref[diagonal : diagonal + 1, 0:half])
    if room > over:
        out_ref[:, 3 * main :] = jnp.zeros((size, 3 * room), BF16)

    def put(k, rows, columns, value):
        for at in (0, 1) if k == 0 else (2,):
            if columns < main:
                out_ref[rows : rows + value.shape[0], at * main + columns : at * main + columns + value.shape[1]] = value
            else:
                start = 3 * main + at * room
                out_ref[rows : rows + value.shape[0], start : start + value.shape[1]] = value

    for k in range(2):
        here = square[k].astype(F32)
        there = turned[:, k * half : (k + 1) * half]
        put(k, 0, 0, jnp.where(row <= col, here, there).astype(BF16))
        end = jnp.broadcast_to(ends[k].astype(F32), (half, half))
        put(k, half, half, jnp.where(row > col, here, jnp.where(row == col, end, there)).astype(BF16))
        put(k, 0, half, side[k])
        put(k, half, 0, turned[:, (2 + k) * half : (3 + k) * half].astype(BF16))
        put(k, 2 * half, 0, stripe[k])
        for j in range(2):
            at = 4 * half + (2 * k + j) * gap
            put(k, j * half, 2 * half, turned[:, at : at + rest].astype(BF16))
    for row_at, take, at, lane in cells:
        corner = split(packed_ref[at : at + take, lane : lane + rest])
        for k in range(2):
            put(k, 2 * half + row_at, 2 * half, corner[k])


def first_kernel(depth, s1_hbm, s2_hbm, gain_hbm, m_hbm, pay, back, m_ref, s2, gain, right, sems):
    here = lax.axis_index("tm")
    width = pay.shape[1]

    @pl.when(here == 0)
    def _():
        load([pltpu.make_async_copy(columns_of(s1_hbm, width, 0), pay, sems.at[0])])

    @pl.when(here == depth - 1)
    def _():
        load(
            [
                pltpu.make_async_copy(m_hbm.at[:, 0, :], m_ref, sems.at[0]),
                pltpu.make_async_copy(columns_of(s2_hbm, width, 0), s2, sems.at[1]),
                pltpu.make_async_copy(columns_of(gain_hbm, width, 0), gain, sems.at[2]),
            ]
        )
        stack_left(back, m_ref[...].T)
        stack_right(right, gain[...] * s2[...])
        pay[...] = dot(back[...], right[...])


def rest_kernel(pieces, depth, after, s1_hbm, s2_hbm, gain_hbm, m_hbm, ahead, back, *rest):
    cut, pay = rest[: 3 * pieces], rest[3 * pieces : 4 * pieces - 1]
    m_ref, held, right, sems = rest[4 * pieces - 1 :]
    here = lax.axis_index("tm")
    width = pay[0].shape[1]
    matrix = pltpu.make_async_copy(m_hbm.at[:, 0, :], m_ref, sems.at[0])
    matrix.start()
    reads = [
        pltpu.make_async_copy(columns_of(source, width, i), held.at[k * pieces + i], sems.at[1 + k * pieces + i])
        for k, source in enumerate((s1_hbm, s2_hbm, gain_hbm))
        for i in range(pieces)
    ]
    writes = [
        pltpu.make_async_copy(held.at[n], target, sems.at[1 + 3 * pieces + n])
        for n, target in enumerate(cut)
    ]
    for copy in reads:
        copy.start()
    matrix.wait()
    stack_left(back, m_ref[...].T)
    stack_left(ahead, m_ref[...])
    for read, write in zip(reads, writes):
        read.wait()
        write.start()

    @pl.when(here == 0)
    def _():
        for i in range(1, pieces):
            pay[i - 1][...] = held[i]

    @pl.when(here == depth - 1)
    def _():
        for i in range(1, pieces):
            stack_right(right, held[2 * pieces + i] * held[pieces + i])
            pay[i - 1][...] = dot(back[...], right[...])

    for write in writes:
        write.wait()


def hop_kernel(stage, depth, at, parts, after, behind, s1_ref, s2_ref, gain_ref, in_ref, ahead_ref, back_ref, *rest):
    edge, pays, (keep_ref, right) = rest[: -parts - 2], rest[-parts - 2 : -2], rest[-2:]
    here = lax.axis_index("tm")
    columns = slice(at, at + in_ref.shape[1])
    width = pays[0].shape[1]

    def send(values):
        for k, pay in enumerate(pays):
            pay[...] = values[:, k * width : (k + 1) * width]

    @pl.when((here == 0) | (here == depth - 1))
    def _():
        keep_ref[...] = in_ref[...]
        if edge:
            send(edge[0][:, columns] if edge[0].shape != in_ref.shape else edge[0][...])

    @pl.when(here == stage)
    def _():
        stack_right(right, in_ref[...])
        state = s1_ref[:, columns] + gain_ref[:, columns] * dot(ahead_ref[...], right[...])
        send(state)
        keep_ref[...] = state

    @pl.when(here == depth - 1 - stage)
    def _():
        swept = s2_ref[:, columns] + in_ref[...]
        keep_ref[...] = swept
        stack_right(right, gain_ref[:, columns] * swept)
        send(dot(back_ref[...], right[...]))


def last_kernel(piece, depth, regions, counts, aliased, final, after, behind, owner_ref, ahead_ref, g_ref, s1_ref, s2_ref, gain_ref, *refs):
    groups = []
    for count in counts:
        groups.append(refs[:count])
        refs = refs[count:]
    *kept, inbox = groups
    before, refs = refs[: 2 * aliased], refs[4 * aliased :]
    f_out, g_out, state, total, right, slots, sems = refs
    here = lax.axis_index("tm")
    size, width = total.shape
    resident = slots.shape[0] == 1

    def copy(source, target, which):
        return pltpu.make_async_copy(source, target, sems.at[which])

    def fetch(which):
        slot = lax.rem(which, 2)
        return copy(g_ref.at[which], slots.at[slot], 2 + slot)

    if not resident:
        fetch(0).start()
    writes = [
        copy(source, columns_of(target, width, piece - 1), 4 + k)
        for k, (source, target) in enumerate(zip(before, (f_out, g_out)))
    ]
    for write in writes:
        write.start()

    def lay(target, sources):
        part = width // len(sources)
        for k, source in enumerate(sources):
            target[:, k * part : (k + 1) * part] = source[...]

    @pl.when(here == 0)
    def _():
        lay(total, inbox)
        state[...] = s1_ref[...]
        total[...] += s2_ref[...]

    for stage in range(1, depth - 1):
        @pl.when(here == stage)
        def _():
            lay(state, kept[stage - 1])
            lay(total, kept[depth - 2 - stage])

    @pl.when(here == depth - 1)
    def _():
        lay(total, inbox)
        stack_right(right, total[...])
        state[...] = s1_ref[...] + gain_ref[...] * dot(ahead_ref[...], right[...])
        total[...] = s2_ref[...]

    if final:
        kept_state = copy(state, columns_of(f_out, width, piece), 0)
        kept_state.start()
    stack_right(right, state[...])
    owners = owner_ref[:, piece * width : (piece + 1) * width]

    def one_owner(owner, carry):
        if resident:
            g = g_ref.at[owner]
        else:
            @pl.when(owner + 1 < regions)
            def _():
                fetch(owner + 1).start()

            fetch(owner).wait()
            g = slots.at[lax.rem(owner, 2)]
        seen = dot(g[...], right[...])
        total[...] += jnp.where(owners == owner, seen, 0.0)
        return carry

    lax.fori_loop(0, regions, one_owner, 0)
    if final:
        load([copy(total, columns_of(g_out, width, piece), 1)])
        kept_state.wait()
    for write in writes:
        write.wait()


def body(search_one, search_two, column_gain, model_matrix, obs_owner, observe_matrix, error_weight, channel_mask):
    depth = lax.axis_size("tm")
    regions = lax.axis_size("region")
    size, columns = search_one.shape[1:]
    channels = observe_matrix.shape[3]
    s1, s2, gain = (far(x.reshape(size, 1, columns)) for x in (search_one, search_two, column_gain))
    matrix = far(model_matrix.reshape(size, 1, size))
    observe = far(observe_matrix.reshape(size, 1, channels))
    pieces = 4
    width = columns // pieces
    deep = stacked(size)
    top = depth - 1
    held = pltpu.VMEM((size, width), F32)
    ones = size * width

    def sent(x, *hops):
        return lax.ppermute(x, "tm", list(hops))

    square = pltpu.VMEM((size, deep), BF16)
    pay = [
        pl.pallas_call(
            functools.partial(first_kernel, depth),
            out_shape=held,
            in_specs=[HBM] * 4,
            out_specs=WHOLE,
            scratch_shapes=[
                square,
                pltpu.VMEM((size, size), F32),
                held,
                held,
                pltpu.VMEM((deep, width), BF16),
                pltpu.SemaphoreType.DMA((3,)),
            ],
            compiler_params=params(10),
            cost_estimate=cost(6 * size * ones, 24 * ones),
            name="first",
        )(s1, s2, gain, matrix)
    ]

    def rest_of(after):
        return pl.pallas_call(
            functools.partial(rest_kernel, pieces, depth),
            out_shape=[square] * 2 + ([held] + [pltpu.HBM((size, width), F32)] * (pieces - 1)) * 3 + [held] * (pieces - 1),
            in_specs=[ANY] + [HBM] * 4,
            out_specs=[WHOLE] * 2 + ([WHOLE] + [HBM] * (pieces - 1)) * 3 + [WHOLE] * (pieces - 1),
            scratch_shapes=[
                pltpu.VMEM((size, size), F32),
                pltpu.VMEM((3 * pieces, size, width), F32),
                pltpu.VMEM((deep, width), BF16),
                pltpu.SemaphoreType.DMA((6 * pieces + 1,)),
            ],
            compiler_params=params(16),
            cost_estimate=cost(6 * size * ones, 24 * ones),
            name="rest",
        )(after, s1, s2, gain, matrix)

    half, rows = packing(size)[0], packing(size)[-1]
    resident = regions % 2 == 0 and regions * size * 2 * deep <= 20 * 1024 * 1024
    def own_operator(after):
        return pl.pallas_call(
            operator_kernel,
            out_shape=pltpu.HBM((regions // 2, rows, 2 * half) if resident else (rows, 2 * half), F32),
            in_specs=[ANY] + [HBM] * 3,
            out_specs=HBM,
            scratch_shapes=[
                pltpu.VMEM((rows, 2 * half), F32),
                pltpu.VMEM((size, channels), F32),
                pltpu.VMEM((1, channels), F32),
                pltpu.VMEM((1, channels), jnp.int32),
                pltpu.VMEM((size, 3 * channels), BF16),
                pltpu.VMEM((size, 3 * channels), BF16),
                pltpu.VMEM((size, size), F32),
                pltpu.SemaphoreType.DMA((max(3, regions // 2),)),
            ],
            compiler_params=params(18),
            cost_estimate=cost(6 * size * size * channels, 8 * size * channels),
            name="operator",
        )(after, observe, far(error_weight[0]), far(channel_mask[0]))

    packed = own_operator(pay[0])
    others = rest_of(far(packed))
    ahead, back, *others = others
    s1s, s2s, gains = ([near(x) for x in others[k * pieces : (k + 1) * pieces]] for k in range(3))
    pay = [*pay, *others[3 * pieces :]]
    ahead, back = near(ahead), near(back)
    length = regions // 2
    turn = pltpu.VMEM((4 * half + 4 * up(size - 2 * half, 16), half), BF16)
    unit = pltpu.VMEM((half, half), BF16)
    shape = (regions, size, deep)

    def unpack(after, blocks, before=None):
        other = before is not None
        return pl.pallas_call(
            functools.partial(unpack_kernel, int(other), size),
            out_shape=[pltpu.VMEM(shape, BF16)] + [pltpu.HBM((rows, 2 * half), F32)] * (length * (not other)),
            in_specs=[ANY] + [ANY if other else HBM] * len(blocks) + [WHOLE] * other,
            out_specs=[WHOLE] + [HBM] * (length * (not other)),
            scratch_shapes=[
                pltpu.VMEM((length, rows, 2 * half), F32),
                turn,
                unit,
                pltpu.SemaphoreType.DMA((2 * length,)),
            ],
            input_output_aliases={1 + len(blocks): 0} if other else {},
            compiler_params=params(8),
            cost_estimate=cost(0, size),
            name="unpack",
        )(after, *map(near if other else far, blocks), *([near(before)] if other else []))

    def unpack_all(after):
        return pl.pallas_call(
            functools.partial(unpack_all_kernel, regions),
            out_shape=pltpu.HBM(shape, BF16),
            in_specs=[ANY, HBM],
            out_specs=HBM,
            scratch_shapes=[
                pltpu.VMEM((2, rows, 2 * half), F32),
                turn,
                unit,
                pltpu.VMEM(shape[1:], BF16),
                pltpu.SemaphoreType.DMA((3,)),
            ],
            compiler_params=params(24),
            cost_estimate=cost(0, regions * size * size * 8),
            name="unpack",
        )(after, far(gathered))

    def hop(after, behind, stage, i, came, at=0, parts=1, *edge, weight=180):
        taken = came.shape[1]
        shape = (size, taken // parts)
        return pl.pallas_call(
            functools.partial(hop_kernel, stage, depth, at, parts),
            out_shape=[pltpu.VMEM(shape, F32)] * parts + [pltpu.VMEM((size, taken), F32)],
            in_specs=[ANY] * 2 + [WHOLE] * (6 + len(edge)),
            out_specs=[WHOLE] * (parts + 1),
            scratch_shapes=[pltpu.VMEM((deep, taken), BF16)],
            compiler_params=params(8),
            cost_estimate=cost(weight * size * size * taken, 24 * size * taken),
            name="hop",
        )(after, behind, s1s[i], s2s[i], gains[i], near(came), ahead, back, *map(near, edge))

    def last(after, behind, i, done):
        groups = [store[stage, i] for stage in range(1, top)] + [[near(x) for x in inbox[i]]]
        operands = [after, behind, obs_owner, ahead, near(operators) if resident else operators, s1s[i], s2s[i], gains[i], *sum(groups, [])]
        specs = [ANY] * 2 + [WHOLE] * (len(operands) - 2)
        if not resident:
            specs[4] = HBM
        aliases = {}
        if done is not None:
            operands += [near(x) for x in done[2:]]
            aliases = {len(operands): 0, len(operands) + 1: 1}
            operands += list(done[:2])
            specs += [WHOLE] * 2 + [HBM] * 2
        final = i == pieces - 1
        slots = (1, 16, LANES) if resident else (2, size, deep)
        return pl.pallas_call(
            functools.partial(last_kernel, i, depth, regions, [len(g) for g in groups], done is not None, final),
            out_shape=[pltpu.HBM((size, 1, columns), F32)] * 2 + ([] if final else [held] * 2),
            in_specs=specs,
            out_specs=[HBM] * 2 + ([] if final else [WHOLE] * 2),
            scratch_shapes=([held] * 2 if final else [])
            + [
                pltpu.VMEM((deep, width), BF16),
                pltpu.VMEM(slots, BF16),
                pltpu.SemaphoreType.DMA((6,)),
            ],
            input_output_aliases=aliases,
            compiler_params=params(8 if resident else 24),
            cost_estimate=cost(size * ones, size * ones),
            name="last",
        )(*operands)

    def link(low, by=1):
        high = top - low
        return [(low, low + by), (high, high - by)]

    both = link(0) + link(2)
    narrow = width // 2
    store, inbox = {}, {i: [] for i in range(pieces)}

    def keep(stage, i, part):
        store.setdefault((stage, i), []).append(near(part))

    def q(after, i, behind=None):
        out, kept = hop(after, after if behind is None else behind, 1, i, arrived[i])
        keep(1, i, kept)
        return sent(out, *link(1, 1 if i < 2 else 2)), kept

    arrived = [sent(pay[i], *link(0)) for i in range(pieces)]
    middle = [None] * pieces
    if resident:
        kinds = [list(range(kind, regions, 2)) for kind in range(2)]
        alike = lax.all_to_all(packed, "region", 0, 0, axis_index_groups=kinds)
    else:
        gathered = lax.all_gather(packed, "region")

    middle[0], after = q(ahead, 0)
    middle[1], after = q(after, 1)
    out, after = hop(after, after, 2, 0, middle[0])
    keep(2, 0, after)
    inbox[0].append(sent(out, *link(2)))
    middle[2], after = q(after, 2)
    middle[3], after = q(after, 3)
    *outs, after = hop(after, inbox[0][0], 2, 1, middle[1], 0, 2, middle[2])
    keep(2, 1, after)
    turned = [sent(out, *both) for out in outs]
    follow = []

    def r2(after, k):
        out, after = hop(after, after, 2, 2, turned[k], k * narrow, 1, middle[3])
        keep(2, 2, after)
        follow.append(sent(out, *both))
        return near(after)

    def r3(after, k):
        out, after = hop(after, after, 2, 3, follow[k], k * narrow, weight=6)
        keep(2, 3, after)
        inbox[3].append(sent(out, *link(2)))
        return near(after)

    if resident:
        operators, *alike = unpack(near(after), [alike])
        others = [lax.ppermute(far(x), "region", [(r, r ^ 1) for r in range(regions)]) for x in alike]
        after = r2(r2(near(operators), 0), 1)
        operators = near(unpack(after, others, operators)[0])
        after = r3(operators, 0)
    else:
        after = r3(r2(r2(after, 0), 1), 0)
        operators = far(unpack_all(after))
    inbox[1] = store[2, 2]
    done = last(after, after, 0, None)
    after = r3(done[3], 1)
    done = last(after, after, 1, done)
    inbox[2] = store[2, 3]
    done = last(done[3], inbox[3][0], 2, done)
    done = last(done[3], done[3], 3, done)[:2]
    return tuple(x.reshape(1, size, columns) for x in done)


def solution(mesh):
    return jax.shard_map(
        body,
        mesh=mesh,
        in_specs=(
            P("tm", None, "region"),
            P("tm", None, "region"),
            P("tm", None, "region"),
            P("tm", None, None),
            P("tm", "region"),
            P("tm", "region", None, None),
            P("tm", "region", None),
            P("tm", "region", None),
        ),
        out_specs=(P("tm", None, "region"), P("tm", None, "region")),
        check_vma=False,
    )
```
